256 devices in a mesh: nodes: 64 (over x, z, core), feat: 4 (over y).
Axes of the slice: x: 4, y: 4, z: 8, core: 2. Of those that a mesh axis runs over, the one named last changes fastest.
Arguments:
- features: bfloat16 [128, 262144], P('feat', 'nodes'), may hold values from -6 to 6
- w_self: bfloat16 [128, 256], replicated, may hold values from -0.5 to 0.5
- w_neigh: bfloat16 [128, 256], replicated, may hold values from -0.5 to 0.5
- hidden_bias: float32 [256], replicated, may hold values from -3 to 3
- cotangent: bfloat16 [256, 262144], P('feat', 'nodes'), may hold values from -0.01171875 to 0.01171875
- hub_local: int32 [64, 32], P('nodes'), may hold values from 0 to 4095
- send_rows: int32 [64, 64, 128], P('nodes'), may hold values from 0 to 4095
- send_count: int32 [64, 64], P('nodes'), may hold values from 0 to 128, as said below
- tile_values: bfloat16 [22528, 128, 128], P('nodes'), may hold values from 0 to 0.039794922
- tile_target: int32 [64, 352], P('nodes'), may hold values from 0 to 31, as said below
- tile_anchor: int32 [64, 352], P('nodes'), may hold values from 0 to 111, as said below
- tile_count: int32 [64], P('nodes'), may hold values from 112 to 352, as said below
Outputs:
- hidden: bfloat16 [256, 262144], P('feat', 'nodes')
- grad_self: float32 [128, 256], P(None, 'feat')
- grad_neigh: float32 [128, 256], P(None, 'feat')
- bias_grad: float32 [256], P('feat')
The draws below stay inside these ranges and needn't reach their ends.
Inputs may be any that keep to these rules, and one draw needn't show every extreme that they name: hub_local[q, j] is the local row of partition q's j-th hub node; hubs are ordered by owner, then by j. send_rows[q, p, j] is the local row of partition q that fills slot j of what q sends to p; slots at or after send_count[q, p] are padding. `send_count`: A partition sends nothing to itself, and every partition fills all 128 slots for at least one other partition. `tile_target`: A block is 128 consecutive local nodes. On every partition each block is the destination of some live tile. `tile_anchor`: A block is 128 consecutive rows of source_p. On every partition each source block that holds halo or hub rows is used by some live tile. Tile slots at or after tile_count[p] are padding: their tile_values, tile_target and tile_anchor entries are arbitrary and must be ignored. Some partition fills all 352 slots.
All inputs are finite; a program needn't handle non-finite values.
Results may differ from the reference program's by a relative error of at most 0.0055.
Values may be sent and summed in bfloat16 or wider, within the bound.
A program may use at most 64 MiB of HBM per device.

```python
import jax
import jax.numpy as jnp
from jax import lax

F_IN = 128
HID = 256
NP = 4096
SLOT = 128
HUB_DEV = 32
TB = 128
NODES = 262144
SOURCE = 14336
BASE_TILES = 112
TILES = 352
N_NODES = 64


def tile_layout(key):
    keys = jax.random.split(jax.random.fold_in(key, 41), 6)
    local_blocks = NP // TB
    source_blocks = SOURCE // TB
    spare = TILES - BASE_TILES
    first_target = jnp.broadcast_to(jnp.arange(local_blocks, dtype=jnp.int32)[None, :], (N_NODES, local_blocks))
    other_target = jax.random.randint(keys[0], (N_NODES, BASE_TILES - local_blocks), 0, local_blocks, dtype=jnp.int32)
    spare_target = jax.random.randint(keys[1], (N_NODES, spare), 0, local_blocks, dtype=jnp.int32)
    targets = jnp.concatenate([first_target, other_target, spare_target], axis=1)
    first_anchor = jax.random.randint(keys[2], (N_NODES, local_blocks), 0, local_blocks, dtype=jnp.int32)
    other_anchor = jnp.broadcast_to(jnp.arange(local_blocks, source_blocks, dtype=jnp.int32)[None, :], (N_NODES, source_blocks - local_blocks))
    spare_anchor = jax.random.randint(keys[3], (N_NODES, spare), 0, source_blocks, dtype=jnp.int32)
    anchors = jnp.concatenate([first_anchor, other_anchor, spare_anchor], axis=1)
    level = jax.random.randint(keys[4], (N_NODES,), 0, 1001, dtype=jnp.int32)
    chosen = jax.random.randint(keys[5], (), 0, N_NODES, dtype=jnp.int32)
    level = jnp.where(jnp.arange(N_NODES, dtype=jnp.int32) == chosen, 1000, level)
    cubed = level * level // 1000 * level // 1000
    counts = BASE_TILES + spare * cubed // 1000
    return (targets, anchors, counts.astype(jnp.int32))


def draw_tile_target(key, part):
    return tile_layout(key)[0]


def draw_tile_anchor(key, part):
    return tile_layout(key)[1]


def draw_tile_count(key, part):
    return tile_layout(key)[2]


def draw_send_count(key, part):
    counts = jax.random.randint(jax.random.fold_in(key, 17), (N_NODES, N_NODES), SLOT // 4, SLOT + 1, dtype=jnp.int32)
    senders = lax.broadcasted_iota(jnp.int32, (N_NODES, N_NODES), 0)
    takers = lax.broadcasted_iota(jnp.int32, (N_NODES, N_NODES), 1)
    counts = jnp.where(takers == (senders + 1) % N_NODES, SLOT, counts)
    counts = jnp.where(senders == takers, 0, counts)
    return counts


def set_ends(drawn, stream_key, smallest, top_value):
    shape = drawn.shape
    spot = [jax.random.randint(jax.random.fold_in(stream_key, axis), (), 0, shape[axis]) for axis in range(len(shape))]
    drawn = drawn.at[tuple(spot)].set(smallest)
    longest = shape.index(max(shape))
    spot[longest] = (spot[longest] + 1) % shape[longest]
    return drawn.at[tuple(spot)].set(top_value)


def shard_levels(rng, dims, pieces, low, top_value):
    gain, own = 1.0, jax.random.fold_in(rng, 6)
    for axis_at, shards_of in pieces:
        steps = jnp.exp(jax.random.uniform(jax.random.fold_in(own, axis_at), (shards_of,), jnp.float32, low / len(pieces), top_value / len(pieces)))
        gain = gain * jnp.repeat(steps, dims[axis_at] // shards_of).reshape([-1 if axis == axis_at else 1 for axis in range(len(dims))])
    return gain


def centred(rng, dims, width, most, cuts=(), kind=jnp.bfloat16):
    loudness = shard_levels(rng, dims, cuts, -0.22, 0.18) if cuts else 1.0
    values = jax.random.normal(rng, dims, jnp.float32) * width * loudness
    return jnp.minimum(jnp.maximum(values, -most), most).astype(kind)


def setup_inputs(seed: int = 0) -> dict:
    splits = jax.random.split(jax.random.key(seed), 13)
    return {
        "features": centred(splits[0], (F_IN, NODES), 1.0, 6.0, ((0, 4), (1, 64))),
        "w_self": centred(splits[1], (F_IN, HID), F_IN ** -0.5, 0.5),
        "w_neigh": centred(splits[2], (F_IN, HID), F_IN ** -0.5, 0.5),
        "hidden_bias": centred(splits[3], (HID,), 0.5, 3.0, (), jnp.float32),
        "cotangent": centred(splits[4], (HID, NODES), (1.0 / NODES ** 0.5), 0.01171875, ((0, 4), (1, 64))),
        "hub_local": set_ends(jax.random.randint(splits[5], (N_NODES, HUB_DEV), 0, NP), jax.random.fold_in(splits[5], 1), 0, NP - 1).astype(jnp.int32),
        "send_rows": set_ends(jax.random.randint(splits[6], (N_NODES, N_NODES, SLOT), 0, NP), jax.random.fold_in(splits[6], 1), 0, NP - 1).astype(jnp.int32),
        "send_count": draw_send_count(jax.random.fold_in(splits[12], 71), 0),
        "tile_values": jnp.clip(0.039794922 * jax.random.uniform(splits[8], (N_NODES * TILES, TB, TB), jnp.float32) ** shard_levels(splits[8], (N_NODES * TILES, TB, TB), ((0, 64),), -0.2, 0.2), 0.0, 0.039794922).astype(jnp.bfloat16),
        "tile_target": draw_tile_target(jax.random.fold_in(splits[12], 71), 0),
        "tile_anchor": draw_tile_anchor(jax.random.fold_in(splits[12], 71), 0),
        "tile_count": draw_tile_count(jax.random.fold_in(splits[12], 71), 0),
    }


def reference(features, w_self, w_neigh, hidden_bias, cotangent, hub_local, send_rows, send_count, tile_values, tile_target, tile_anchor, tile_count):
    owner_base = jnp.arange(N_NODES, dtype=jnp.int32)[:, None] * NP
    hub_index = (owner_base + hub_local).reshape(-1).astype(jnp.int32)
    hub_rows = jnp.take(features, hub_index, axis=1)
    slot_index = lax.broadcasted_iota(jnp.int32, (N_NODES, SLOT), 1)
    local_blocks = NP // TB
    block_ids = jnp.arange(local_blocks, dtype=jnp.int32)

    def one_part(part_index):
        own_rows = lax.dynamic_slice_in_dim(features, (part_index * NP).astype(jnp.int32), NP, 1)
        sent_rows = jnp.take(send_rows, part_index, axis=1)
        live_slot = slot_index < jnp.take(send_count, part_index, axis=1)[:, None]
        halo_rows = jnp.take(features, (owner_base + sent_rows).reshape(-1).astype(jnp.int32), axis=1)
        halo_rows = jnp.where(live_slot.reshape(1, -1), halo_rows, jnp.zeros_like(halo_rows))
        source_rows = jnp.concatenate([own_rows, halo_rows, hub_rows], axis=1).reshape(F_IN, SOURCE // TB, TB)
        tile_block = lax.dynamic_slice_in_dim(tile_values, (part_index * TILES).astype(jnp.int32), TILES, 0).astype(jnp.float32)
        targets = jnp.take(tile_target, part_index, axis=0)
        anchors = jnp.take(tile_anchor, part_index, axis=0)
        live_tiles = jnp.arange(TILES, dtype=jnp.int32) < jnp.take(tile_count, part_index)
        picked = jnp.take(source_rows, anchors, axis=1).astype(jnp.float32)
        products = jnp.einsum("ftk,tik->fti", picked, tile_block, precision=lax.Precision.HIGHEST)
        selector = ((targets[:, None] == block_ids[None, :]) & live_tiles[:, None]).astype(jnp.float32)
        summed = jnp.einsum("fti,tn->fni", products, selector, precision=lax.Precision.HIGHEST)
        return summed.reshape(F_IN, NP).astype(jnp.bfloat16)

    per_part = lax.map(one_part, jnp.arange(N_NODES, dtype=jnp.int32))
    aggregate = jnp.transpose(per_part, (1, 0, 2)).reshape(F_IN, NP * N_NODES)
    contract_first = (((0,), (0,)), ((), ()))
    contract_last = (((1,), (1,)), ((), ()))
    preact = lax.dot_general(w_self, features, contract_first, preferred_element_type=jnp.float32)
    preact = preact + lax.dot_general(w_neigh, aggregate, contract_first, preferred_element_type=jnp.float32)
    preact = preact + hidden_bias[:, None]
    sigmoid_value = jax.nn.sigmoid(preact)
    hidden = (preact * sigmoid_value).astype(jnp.bfloat16)
    pre_grad = (cotangent.astype(jnp.float32) * sigmoid_value * (1.0 + preact * (1.0 - sigmoid_value))).astype(jnp.bfloat16)
    grad_self = lax.dot_general(features, pre_grad, contract_last, preferred_element_type=jnp.float32)
    grad_neigh = lax.dot_general(aggregate, pre_grad, contract_last, preferred_element_type=jnp.float32)
    bias_grad = jnp.sum(pre_grad.astype(jnp.float32), axis=1)
    return hidden, grad_self, grad_neigh, bias_grad
```

```python
import functools

import jax
import jax.numpy as jnp
from jax import lax
from jax.experimental import pallas as pl
from jax.experimental.pallas import tpu as pltpu
from jax.sharding import PartitionSpec as P

MESH = pl.DeviceIdType.MESH
NX, NZ, NN, NF = 4, 8, 64, 4
CHIPS = NX * NZ
VMEM = pl.BlockSpec(memory_space=pltpu.VMEM)
SMEM = pl.BlockSpec(memory_space=pltpu.SMEM)
TILES_STEP = 32
F32 = jnp.float32
BF16 = jnp.bfloat16


def greet(me, feat):
    barrier = pltpu.get_barrier_semaphore()

    def node(k, _):
        pl.semaphore_signal(
            barrier, inc=1, device_id={"nodes": (me + k) % NN, "feat": feat}, device_id_type=MESH
        )
        return 0

    lax.fori_loop(1, NN, node, 0)
    for k in range(1, NF):
        pl.semaphore_signal(
            barrier, inc=1, device_id={"nodes": me, "feat": (feat + k) % NF}, device_id_type=MESH
        )
    return barrier


def exchange_kernel(
    feat_ref, idx_ref, src_ref, full_ref, stacked, outbox, hub0, hub0_in, hub1, hub1_in,
    halo_send, halo_recv, feat_send, feat_recv, hub_send, hub_recv,
):
    me = lax.axis_index("nodes")
    feat = lax.axis_index("feat")
    core = me % 2
    z = (me // 2) % NZ
    x = me // (2 * NZ)
    barrier = greet(me, feat)

    for h in range(16):
        stacked[h * 32 : (h + 1) * 32, :] = feat_ref[:, h * 256 : (h + 1) * 256]

    def pick(row):
        index = idx_ref[pl.ds(row, 1), :]
        low = index & 255
        high = index >> 8
        hot = (lax.broadcasted_iota(jnp.int32, (256, 256), 0) == low).astype(F32).astype(BF16)
        parts = jnp.dot(stacked[...], hot, preferred_element_type=F32)
        out = jnp.zeros((32, 256), F32)
        for h in range(16):
            out = jnp.where(high == h, parts[h * 32 : (h + 1) * 32], out)
        return out.astype(BF16)

    hub0[...] = pick(CHIPS)[:, :128]
    pl.semaphore_wait(barrier, NN - 1 + NF - 1)

    def send(src, dst, send_sem, recv_sem, node, part):
        copy = pltpu.make_async_remote_copy(
            src_ref=src, dst_ref=dst, send_sem=send_sem, recv_sem=recv_sem,
            device_id={"nodes": node, "feat": part}, device_id_type=MESH,
        )
        copy.start()
        return copy

    sibling = me + 1 - 2 * core
    first = send(hub0, hub0_in, hub_send.at[0], hub_recv.at[0], sibling, feat)
    feat_copies = [
        send(feat_ref, full_ref.at[feat], feat_send.at[k], feat_recv.at[k], me, (feat + k) % NF)
        for k in range(1, NF)
    ]

    def halo_copy(node):
        return pltpu.make_async_remote_copy(
            src_ref=outbox.at[node], dst_ref=src_ref.at[32 + me],
            send_sem=halo_send.at[node], recv_sem=halo_recv.at[me],
            device_id={"nodes": node, "feat": feat}, device_id_type=MESH,
        )

    def step(i, _):
        turn = i % NZ
        dx = i // NZ
        dz = (4 + (1 - 2 * (turn % 2)) * ((turn + 1) // 2)) % NZ
        chip = ((x + dx) % NX) * NZ + (z + dz) % NZ
        rows = pick(chip)
        outbox[2 * chip] = rows[:, :128]
        outbox[2 * chip + 1] = rows[:, 128:]
        halo_copy(2 * chip).start()
        halo_copy(2 * chip + 1).start()
        return 0

    def own_chip():
        chip = me // 2
        rows = pick(chip)
        outbox[2 * chip] = rows[:, :128]
        outbox[2 * chip + 1] = rows[:, 128:]
        halo_copy(sibling).start()
        src_ref[32 + me] = jnp.zeros((32, 128), BF16)

    own_chip()
    lax.fori_loop(0, 3, step, 0)
    first.wait()
    hub1[...] = hub0[...] + hub0_in[...]
    across = x * 2 * NZ + (z + 1 - 2 * (z % 2)) * 2 + core
    second = send(hub1, hub1_in, hub_send.at[1], hub_recv.at[1], across, feat)
    lax.fori_loop(3, 7, step, 0)
    second.wait()
    block = 96 + me // 4
    src_ref[block] = hub1[...] + hub1_in[...]
    along_z = [
        send(
            src_ref.at[block], src_ref.at[block], hub_send.at[1 + k], hub_recv.at[1 + k],
            x * 2 * NZ + ((z + 2 * k) % NZ) * 2 + core, feat,
        )
        for k in range(1, 4)
    ]
    lax.fori_loop(8, 18, step, 0)
    for copy in along_z:
        copy.wait()
    group = src_ref.at[pl.ds(96 + x * 4, 4)]
    along_x = [
        send(
            group, group, hub_send.at[4 + k], hub_recv.at[4 + k],
            ((x + k) % NX) * 2 * NZ + z * 2 + core, feat,
        )
        for k in range(1, 4)
    ]
    lax.fori_loop(18, 32, step, 0)
    for b in range(32):
        src_ref[b] = feat_ref[:, b * 128 : (b + 1) * 128]
    full_ref[feat] = feat_ref[...]
    for copy in along_x:
        copy.wait()
    for copy in feat_copies:
        copy.wait()

    def arrived(k, _):
        node = (me + k) % NN
        pltpu.make_async_remote_copy(
            src_ref=outbox.at[node], dst_ref=src_ref.at[32 + node],
            send_sem=halo_send.at[node], recv_sem=halo_recv.at[node],
            device_id={"nodes": node, "feat": feat}, device_id_type=MESH,
        ).wait()
        return 0

    lax.fori_loop(1, NN, arrived, 0)


def exchange(features, index):
    cols = features.shape[1]
    return pl.pallas_call(
        exchange_kernel,
        name="exchange",
        out_shape=(
            jax.ShapeDtypeStruct((112, 32, 128), BF16),
            jax.ShapeDtypeStruct((NF, 32, cols), BF16),
        ),
        in_specs=[VMEM, VMEM],
        out_specs=(VMEM, VMEM),
        scratch_shapes=[
            pltpu.VMEM((512, 256), BF16),
            pltpu.VMEM((NN, 32, 128), BF16),
            pltpu.VMEM((32, 128), BF16),
            pltpu.VMEM((32, 128), BF16),
            pltpu.VMEM((32, 128), BF16),
            pltpu.VMEM((32, 128), BF16),
            pltpu.SemaphoreType.DMA((NN,)),
            pltpu.SemaphoreType.DMA((NN,)),
            pltpu.SemaphoreType.DMA((NF,)),
            pltpu.SemaphoreType.DMA((NF,)),
            pltpu.SemaphoreType.DMA((8,)),
            pltpu.SemaphoreType.DMA((8,)),
        ],
        compiler_params=pltpu.CompilerParams(
            collective_id=0, has_side_effects=True, vmem_limit_bytes=32 * 2**20
        ),
    )(features, index)


def tiles_kernel(count, targets, anchors, values_ref, src_ref, out_ref, sums):
    turn = pl.program_id(0)
    lanes = sums.shape[0]

    @pl.when(turn == 0)
    def _():
        sums[...] = jnp.zeros_like(sums)

    live = count[0]

    def batch(b, _):
        first = b * 16
        products = []
        spots = []
        for j in range(16):
            slot = turn * TILES_STEP + first + j
            block = jnp.clip(anchors[0, slot], 0, 111)
            product = lax.dot_general(
                src_ref[block], values_ref[first + j], (((1,), (1,)), ((), ())),
                preferred_element_type=F32,
            )
            products.append(jnp.where(slot < live, product, 0.0))
            spots.append(jnp.clip(targets[0, slot], 0, 31))
        for j in range(16):
            sums[j % lanes, spots[j]] += products[j]
        return 0

    lax.fori_loop(0, TILES_STEP // 16, batch, 0)

    @pl.when(turn == pl.num_programs(0) - 1)
    def _():
        for d in range(32):
            total = sums[0, d]
            for lane in range(1, lanes):
                total = total + sums[lane, d]
            out_ref[:, d * 128 : (d + 1) * 128] = total.astype(BF16)


def tile_sums(count, targets, anchors, values, source):
    steps = values.shape[0] // TILES_STEP
    return pl.pallas_call(
        tiles_kernel,
        name="tile_sums",
        grid_spec=pltpu.PrefetchScalarGridSpec(
            num_scalar_prefetch=3,
            grid=(steps,),
            in_specs=[
                pl.BlockSpec((TILES_STEP, 128, 128), lambda i, *_: (i, 0, 0)),
                VMEM,
            ],
            out_specs=pl.BlockSpec((32, 4096), lambda i, *_: (0, 0)),
            scratch_shapes=[pltpu.VMEM((4, 32, 32, 128), F32)],
        ),
        out_shape=jax.ShapeDtypeStruct((32, 4096), BF16),
        compiler_params=pltpu.CompilerParams(vmem_limit_bytes=32 * 2**20),
    )(count, targets, anchors, values, source)


def layer_kernel(
    agg_ref, full_ref, wself_ref, wneigh_ref, bias_ref, cot_ref,
    hidden_ref, gself_ref, gneigh_ref, gbias_ref,
    aggs, weights, bias, sums, pieces, inbox, totals,
    agg_send, agg_recv, piece_send, piece_recv, total_send, total_recv,
):
    me = lax.axis_index("nodes")
    feat = lax.axis_index("feat")
    barrier = greet(me, feat)

    def mine(ref):
        part = ref[:, 0:64]
        for k in range(1, NF):
            part = jnp.where(feat == k, ref[:, k * 64 : (k + 1) * 64], part)
        return part

    weights[0] = mine(wself_ref).T
    weights[1] = mine(wneigh_ref).T
    bias[...] = jnp.broadcast_to(mine(bias_ref), (128, 64)).T
    aggs[feat] = agg_ref[...]
    sums[...] = jnp.zeros_like(sums)
    pieces[16] = jnp.zeros((8, 128), F32)
    pl.semaphore_wait(barrier, NN - 1 + NF - 1)

    copies = []
    for k in range(1, NF):
        copy = pltpu.make_async_remote_copy(
            src_ref=agg_ref, dst_ref=aggs.at[feat],
            send_sem=agg_send.at[k], recv_sem=agg_recv.at[k],
            device_id={"nodes": me, "feat": (feat + k) % NF}, device_id_type=MESH,
        )
        copy.start()
        copies.append(copy)
    for copy in copies:
        copy.wait()

    last = (((1,), (1,)), ((), ()))
    width = 512

    def columns(c, _):
        span = pl.ds(pl.multiple_of(c * width, width), width)
        own = full_ref[:, :, span].reshape(128, width)
        neigh = aggs[:, :, span].reshape(128, width)
        pre = jnp.dot(weights[0], own, preferred_element_type=F32)
        pre = pre + jnp.dot(weights[1], neigh, preferred_element_type=F32)
        pre = pre + bias[:, 0:1]
        gate = jax.nn.sigmoid(pre)
        hidden_ref[:, span] = (pre * gate).astype(BF16)
        grad = (cot_ref[:, span].astype(F32) * gate * (1.0 + pre * (1.0 - gate))).astype(BF16)
        sums[0:128, :] += lax.dot_general(own, grad, last, preferred_element_type=F32)
        sums[128:256, :] += lax.dot_general(neigh, grad, last, preferred_element_type=F32)
        sums[256:264, :] += lax.dot_general(
            jnp.ones((8, width), BF16), grad, last, preferred_element_type=F32
        )
        return 0

    lax.fori_loop(0, cot_ref.shape[1] // width, columns, 0)

    for r in range(16):
        pieces[r] = jnp.concatenate(
            [sums[8 * r : 8 * r + 8, :], sums[128 + 8 * r : 136 + 8 * r, :]], axis=1
        )
    pieces[16, :, 0:64] = sums[256:264, :]

    def piece_copy(r):
        return pltpu.make_async_remote_copy(
            src_ref=pieces.at[r], dst_ref=inbox.at[me],
            send_sem=piece_send.at[r], recv_sem=piece_recv.at[me],
            device_id={"nodes": 3 * r, "feat": feat}, device_id_type=MESH,
        )

    def total_copy(r, node):
        return pltpu.make_async_remote_copy(
            src_ref=totals.at[r], dst_ref=totals.at[r],
            send_sem=total_send.at[node], recv_sem=total_recv.at[r],
            device_id={"nodes": node, "feat": feat}, device_id_type=MESH,
        )

    for r in range(17):

        @pl.when(me != 3 * r)
        def _():
            piece_copy(r).start()

    reducer = jnp.logical_and(me % 3 == 0, me <= 48)

    @pl.when(reducer)
    def _():
        r = me // 3
        inbox[me] = pieces[r]

        def arrived(k, _):
            node = (me + k) % NN
            pltpu.make_async_remote_copy(
                src_ref=pieces.at[r], dst_ref=inbox.at[node],
                send_sem=piece_send.at[r], recv_sem=piece_recv.at[node],
                device_id={"nodes": node, "feat": feat}, device_id_type=MESH,
            ).wait_recv()
            return 0

        lax.fori_loop(1, NN, arrived, 0)
        totals[r] = jnp.sum(inbox[...], axis=0)

        def give(k, _):
            total_copy(r, (me + k) % NN).start()
            return 0

        lax.fori_loop(1, NN, give, 0)

        def given(k, _):
            total_copy(r, (me + k) % NN).wait_send()
            return 0

        lax.fori_loop(1, NN, given, 0)

    for r in range(17):

        @pl.when(me != 3 * r)
        def _():
            piece_copy(r).wait_send()
            total_copy(r, 3 * r).wait_recv()

    for r in range(16):
        gself_ref[8 * r : 8 * r + 8, :] = totals[r, :, 0:64]
        gneigh_ref[8 * r : 8 * r + 8, :] = totals[r, :, 64:128]
    gbias_ref[...] = totals[16, 0:1, 0:64]


def layer(agg, full, w_self, w_neigh, bias, cotangent):
    cols = cotangent.shape[1]
    return pl.pallas_call(
        layer_kernel,
        name="layer",
        out_shape=(
            jax.ShapeDtypeStruct((64, cols), BF16),
            jax.ShapeDtypeStruct((128, 64), F32),
            jax.ShapeDtypeStruct((128, 64), F32),
            jax.ShapeDtypeStruct((1, 64), F32),
        ),
        in_specs=[VMEM] * 6,
        out_specs=(VMEM,) * 4,
        scratch_shapes=[
            pltpu.VMEM((NF, 32, cols), BF16),
            pltpu.VMEM((2, 64, 128), BF16),
            pltpu.VMEM((64, 128), F32),
            pltpu.VMEM((264, 64), F32),
            pltpu.VMEM((17, 8, 128), F32),
            pltpu.VMEM((NN, 8, 128), F32),
            pltpu.VMEM((17, 8, 128), F32),
            pltpu.SemaphoreType.DMA((NF,)),
            pltpu.SemaphoreType.DMA((NF,)),
            pltpu.SemaphoreType.DMA((17,)),
            pltpu.SemaphoreType.DMA((NN,)),
            pltpu.SemaphoreType.DMA((NN,)),
            pltpu.SemaphoreType.DMA((17,)),
        ],
        compiler_params=pltpu.CompilerParams(
            collective_id=1, has_side_effects=True, vmem_limit_bytes=32 * 2**20
        ),
    )(agg, full, w_self, w_neigh, bias, cotangent)


def local(
    features, w_self, w_neigh, hidden_bias, cotangent, hub_local, send_rows, send_count,
    tile_values, tile_target, tile_anchor, tile_count,
):
    me = lax.axis_index("nodes")
    slots = lax.broadcasted_iota(jnp.int32, (NN, 128), 1)
    rows = jnp.where(slots < send_count[0][:, None], send_rows[0], -1).reshape(CHIPS, 256)
    lane = lax.broadcasted_iota(jnp.int32, (1, 256), 1)
    hubs = jnp.where(lane // 32 == me % 4, jnp.tile(hub_local, (1, 8)), -1)
    index = jnp.concatenate([rows, hubs], axis=0)
    source, full = exchange(features, index)
    agg = tile_sums(tile_count, tile_target, tile_anchor, tile_values, source)
    hidden, grad_self, grad_neigh, bias_grad = layer(
        agg, full, w_self, w_neigh, hidden_bias.reshape(1, -1), cotangent
    )
    return hidden, grad_self, grad_neigh, bias_grad.reshape(-1)


def solution(mesh):
    in_specs = (
        P("feat", "nodes"), P(), P(), P(), P("feat", "nodes"), P("nodes", None),
        P("nodes", None, None), P("nodes", None), P("nodes", None, None), P("nodes", None),
        P("nodes", None), P("nodes"),
    )
    out_specs = (P("feat", "nodes"), P(None, "feat"), P(None, "feat"), P("feat"))
    return jax.shard_map(local, mesh=mesh, in_specs=in_specs, out_specs=out_specs, check_vma=False)
```

```python
import jax
import jax.numpy as jnp
from jax import lax
from jax.experimental import pallas as pl
from jax.experimental.pallas import tpu as pltpu
from jax.sharding import PartitionSpec as P

MESH = pl.DeviceIdType.MESH
NX, NZ, NN, NF = 4, 8, 64, 4
TILES = 352
BLOCKS = 32
UNROLL = 32
PARTS = 8
LAST = (((1,), (1,)), ((), ()))
F32 = jnp.float32
BF16 = jnp.bfloat16
I32 = jnp.int32


def peer_signal(barrier, node, part):
    pl.semaphore_signal(
        barrier, inc=1, device_id={"nodes": node, "feat": part}, device_id_type=MESH
    )


def remote(src, dst, send_sem, recv_sem, node, part):
    return pltpu.make_async_remote_copy(
        src_ref=src, dst_ref=dst, send_sem=send_sem, recv_sem=recv_sem,
        device_id={"nodes": node, "feat": part}, device_id_type=MESH,
    )


def started(copy):
    copy.start()
    return copy


def layer_kernel(
    feat_in, wself_in, wneigh_in, bias_in, cot_in, hub_in, rows_in, count_in, values_in, target_in,
    anchor_in, live_in, hidden_ref, gself_ref, gneigh_ref, gbias_ref,
    feat_ref, wself_ref, wneigh_ref, bias_ref, cot_ref, hub_ref, rows_ref, count_ref, values_ref,
    target_ref, anchor_ref, live_ref,
    src_ref, full_ref, stacked, outbox, hub0, hub0_in, hub1, hub1_in, table, order, running,
    aggs, weights, bias, own_term, sums, pieces, inbox, partial, crossbox, totals,
    load_sem, table_sem, halo_send, halo_recv, feat_send, feat_recv, hub_send, hub_recv,
    agg_send, agg_recv, reduce_send, reduce_recv,
):
    me = lax.axis_index("nodes")
    feat = lax.axis_index("feat")
    core = me % 2
    z = (me // 2) % NZ
    x = me // (2 * NZ)
    loads = [
        started(pltpu.make_async_copy(src, dst, load_sem.at[i]))
        for i, (src, dst) in enumerate(
            (
                (feat_in, feat_ref), (rows_in, rows_ref), (hub_in, hub_ref), (count_in, count_ref),
                (target_in, target_ref), (anchor_in, anchor_ref), (live_in, live_ref),
                (wself_in, wself_ref), (wneigh_in, wneigh_ref), (bias_in, bias_ref),
                (cot_in, cot_ref), (values_in, values_ref),
            )
        )
    ]
    barrier = pltpu.get_barrier_semaphore()

    def node_signal(k, _):
        peer_signal(barrier, (me + k) % NN, feat)
        return 0

    lax.fori_loop(1, NN, node_signal, 0)
    for k in range(1, NF):
        peer_signal(barrier, me, (feat + k) % NF)

    for copy in loads[:4]:
        copy.wait()
    for h in range(16):
        stacked[h * 32 : (h + 1) * 32, :] = feat_ref[:, h * 256 : (h + 1) * 256]
    lane = lax.broadcasted_iota(I32, (1, 128), 1)

    def pick(index):
        low = index & 255
        high = index >> 8
        hot = (lax.broadcasted_iota(I32, (256, 256), 0) == low).astype(F32).astype(BF16)
        parts = jnp.dot(stacked[...], hot, preferred_element_type=F32)
        out = jnp.zeros((32, 256), F32)
        for h in range(16):
            out = jnp.where(high == h, parts[h * 32 : (h + 1) * 32], out)
        return out.astype(BF16)

    def fill(chip):
        first = jnp.where(lane < count_ref[0, 2 * chip], rows_ref[pl.ds(2 * chip, 1), :], -1)
        second = jnp.where(
            lane < count_ref[0, 2 * chip + 1], rows_ref[pl.ds(2 * chip + 1, 1), :], -1
        )
        rows = pick(jnp.concatenate([first, second], axis=1))
        outbox[2 * chip] = rows[:, :128]
        outbox[2 * chip + 1] = rows[:, 128:]

    def halo_copy(node):
        return remote(
            outbox.at[node], src_ref.at[32 + me], halo_send.at[node], halo_recv.at[me], node, feat
        )

    def chip_at(k, dz):
        dx = 2 + (1 - 2 * (k % 2)) * ((k + 1) // 2)
        return ((x + dx) % NX) * NZ + (z + dz) % NZ

    def send(chip):
        halo_copy(2 * chip).start()
        halo_copy(2 * chip + 1).start()

    def opposite(k, _):
        fill(chip_at(k, 4))
        return 0

    def opposite_send(k, _):
        send(chip_at(k, 4))
        return 0

    def between(j, _):
        turn = j % 8
        dz = 4 + (2 * (turn % 2) - 1) * (1 + j // 8)
        chip = chip_at(turn // 2, dz)
        fill(chip)
        send(chip)
        return 0

    def level(k, _):
        chip = chip_at(k, 0)
        fill(chip)
        send(chip)
        return 0

    sibling = me + 1 - 2 * core
    hubs = jnp.concatenate([hub_ref[...]] * 4, axis=1)
    hubs = jnp.where(lane // 32 == me % 4, hubs, -1)
    hub0[...] = pick(jnp.concatenate([hubs, jnp.full_like(hubs, -1)], axis=1))[:, :128]
    src_ref[32 + me] = jnp.zeros((32, 128), BF16)
    lax.fori_loop(0, 4, opposite, 0)
    pl.semaphore_wait(barrier, NN - 1 + NF - 1)

    first = started(remote(hub0, hub0_in, hub_send.at[0], hub_recv.at[0], sibling, feat))
    feat_copies = [
        started(
            remote(
                feat_ref, full_ref.at[feat], feat_send.at[k], feat_recv.at[k], me,
                (feat + k) % NF,
            )
        )
        for k in range(1, NF)
    ]
    lax.fori_loop(0, 4, opposite_send, 0)
    lax.fori_loop(0, 2, between, 0)
    first.wait()
    hub1[...] = hub0[...] + hub0_in[...]
    across_pair = x * 2 * NZ + (z + 1 - 2 * (z % 2)) * 2 + core
    second = started(remote(hub1, hub1_in, hub_send.at[1], hub_recv.at[1], across_pair, feat))
    lax.fori_loop(2, 9, between, 0)
    second.wait()
    block = 96 + me // 4
    src_ref[block] = hub1[...] + hub1_in[...]
    along_z = [
        started(
            remote(
                src_ref.at[block], src_ref.at[block], hub_send.at[1 + k], hub_recv.at[1 + k],
                x * 2 * NZ + ((z + 2 * k) % NZ) * 2 + core, feat,
            )
        )
        for k in range(1, 4)
    ]
    lax.fori_loop(9, 22, between, 0)
    for copy in along_z:
        copy.wait()
    group_blocks = src_ref.at[pl.ds(96 + x * 4, 4)]
    along_x = [
        started(
            remote(
                group_blocks, group_blocks, hub_send.at[4 + k], hub_recv.at[4 + k],
                ((x + k) % NX) * 2 * NZ + z * 2 + core, feat,
            )
        )
        for k in range(1, 4)
    ]
    lax.fori_loop(22, 24, between, 0)
    lax.fori_loop(0, 3, level, 0)
    fill(me // 2)
    halo_copy(sibling).start()

    for copy in loads[4:]:
        copy.wait()
    down = lax.broadcasted_iota(I32, (TILES, TILES), 0)
    along = lax.broadcasted_iota(I32, (TILES, TILES), 1)
    slot_row = lax.broadcasted_iota(I32, (1, TILES), 1)
    key_row = jnp.where(slot_row < live_ref[0], jnp.clip(target_ref[...], 0, BLOCKS - 1), BLOCKS)
    anchor_row = jnp.clip(anchor_ref[...], 0, 111)

    def column(row):
        return jnp.sum(jnp.where(down == along, row, 0), axis=1, keepdims=True)

    key = column(key_row)
    ahead = (key_row < key) | ((key_row == key) & (along < down))
    rank = jnp.sum(jnp.where(ahead, 1, 0), axis=1, keepdims=True)
    placed = rank == along

    def sorted_row(col):
        return jnp.sum(jnp.where(placed, col, 0), axis=0, keepdims=True)

    key_sorted = sorted_row(key)
    slot_col = lax.broadcasted_iota(I32, (TILES, 1), 0)
    table[0:1, 0:TILES] = sorted_row(slot_col)
    table[1:2, 0:TILES] = sorted_row(column(anchor_row))
    table[2:3, 0:TILES] = key_sorted
    blocks_along = lax.broadcasted_iota(I32, (TILES, 128), 1)
    table[3:4, 0:128] = jnp.maximum(
        jnp.sum(jnp.where(key <= blocks_along, 1, 0), axis=0, keepdims=True) - 1, 0
    )
    to_scalars = started(pltpu.make_async_copy(table, order, table_sem))

    def mine(ref):
        part = ref[:, 0:64]
        for k in range(1, NF):
            part = jnp.where(feat == k, ref[:, k * 64 : (k + 1) * 64], part)
        return part

    weights[0] = mine(wself_ref).T
    weights[1] = mine(wneigh_ref).T
    bias[...] = jnp.broadcast_to(mine(bias_ref), (128, 64)).T
    sums[...] = jnp.zeros_like(sums)
    for b in range(32):
        src_ref[b] = feat_ref[:, b * 128 : (b + 1) * 128]
    full_ref[feat] = feat_ref[...]
    to_scalars.wait()
    for copy in along_x:
        copy.wait()

    def arrived(k, _):
        node = (me + k) % NN
        remote(
            outbox.at[node], src_ref.at[32 + node], halo_send.at[node], halo_recv.at[node], node,
            feat,
        ).wait()
        return 0

    lax.fori_loop(1, NN, arrived, 0)

    empty = jnp.zeros((32, 128), BF16)

    def batch(b, total):
        products = []
        for j in range(0, UNROLL, 2):
            slot = b * UNROLL + j
            one = src_ref[order[1, slot]]
            two = src_ref[order[1, slot + 1]]
            rows = jnp.concatenate(
                [jnp.concatenate([one, empty], axis=1), jnp.concatenate([empty, two], axis=1)],
                axis=0,
            )
            pair = jnp.concatenate(
                [values_ref[order[0, slot]], values_ref[order[0, slot + 1]]], axis=1
            )
            product = lax.dot_general(rows, pair, LAST, preferred_element_type=F32)
            products += [product[:32], product[32:]]
        for j in range(UNROLL):
            slot = b * UNROLL + j
            same = order[2, slot] == order[2, jnp.maximum(slot - 1, 0)]
            total = jnp.where(same, total, 0.0) + products[j]
            running[slot] = total
        return total

    lax.fori_loop(0, TILES // UNROLL, batch, jnp.zeros((32, 128), F32))

    width = cot_ref.shape[1] // PARTS

    def at(c):
        return pl.ds(pl.multiple_of(c * width, width), width)

    def direct(c, way):
        slot = (1 - way) // 2
        own = aggs.at[feat, :, at(c)]
        return remote(
            own, own, agg_send.at[slot, c], agg_recv.at[slot, c], me, (feat + way) % NF
        )

    def relay(c):
        way = 1 - 2 * (c % 2)
        theirs = aggs.at[(feat - way) % NF, :, at(c)]
        return remote(
            theirs, theirs, agg_send.at[2, c], agg_recv.at[2, c], me, (feat + way) % NF
        )

    def give(c, _):
        ends = [running[order[3, c * 4 + k]].astype(BF16) for k in range(4)]
        aggs[feat, :, at(c)] = jnp.concatenate(ends, axis=1)
        direct(c, 1).start()
        direct(c, -1).start()
        return 0

    lax.fori_loop(0, PARTS, give, 0)
    for copy in feat_copies:
        copy.wait()

    def own_part(c, _):
        own = full_ref[:, :, at(c)].reshape(128, width)
        own_term[:, at(c)] = (
            jnp.dot(weights[0], own, preferred_element_type=F32) + bias[:, 0:1]
        )
        return 0

    def columns(c):
        span = at(c)
        relay(c).wait()
        own = full_ref[:, :, span].reshape(128, width)
        neigh = aggs[:, :, span].reshape(128, width)
        pre = own_term[:, span] + jnp.dot(weights[1], neigh, preferred_element_type=F32)
        gate = jax.nn.sigmoid(pre)
        hidden_ref[:, span] = (pre * gate).astype(BF16)
        grad = (cot_ref[:, span].astype(F32) * gate * (1.0 + pre * (1.0 - gate))).astype(BF16)
        every = jnp.concatenate([own, neigh, jnp.ones((128, width), BF16)], axis=0)
        sums[...] += lax.dot_general(grad, every, LAST, preferred_element_type=F32)

    def pass_on(c, _):
        direct(c, 1).wait()
        direct(c, -1).wait()
        relay(c).start()
        return 0

    def turn(c, _):
        pass_on(c + 2, 0)
        columns(c)
        return 0

    lax.fori_loop(0, PARTS, own_part, 0)
    lax.fori_loop(0, 2, pass_on, 0)
    lax.fori_loop(0, PARTS - 2, turn, 0)
    columns(PARTS - 2)
    columns(PARTS - 1)

    group = x * 2 + core

    def mate(j):
        return (j // 2) * 2 * NZ + z * 2 + j % 2

    def across(zz):
        return x * 2 * NZ + zz * 2 + core

    for j in range(8):
        pieces[j] = sums[8 * j : 8 * j + 8, :]
    own_piece = pieces.at[group]

    def scatter(k):
        j = (group + k) % 8
        return remote(
            pieces.at[j], inbox.at[group], reduce_send.at[0, j], reduce_recv.at[0, group],
            mate(j), feat,
        )

    def scatter_in(k):
        j = (group + k) % 8
        return remote(
            pieces.at[j], inbox.at[j], reduce_send.at[0, j], reduce_recv.at[0, j], mate(j), feat
        )

    for k in range(1, 8):
        scatter(k).start()
    inbox[group] = own_piece[...]
    for k in range(1, 8):
        scatter_in(k).wait()
    crossed = inbox[0]
    for j in range(1, 8):
        crossed = crossed + inbox[j]
    partial[...] = crossed
    crossbox[z] = crossed

    def cross(k):
        zz = (z + k) % NZ
        return remote(
            partial, crossbox.at[z], reduce_send.at[1, zz], reduce_recv.at[1, z], across(zz), feat
        )

    def cross_in(k):
        zz = (z + k) % NZ
        return remote(
            partial, crossbox.at[zz], reduce_send.at[1, zz], reduce_recv.at[1, zz], across(zz),
            feat,
        )

    for k in range(1, 8):
        cross(k).start()
    for k in range(1, 8):
        cross_in(k).wait()
    total = crossbox[0]
    for j in range(1, 8):
        total = total + crossbox[j]
    totals[group] = total

    def spread(k):
        j = (group + k) % 8
        return remote(
            totals.at[group], totals.at[group], reduce_send.at[2, j], reduce_recv.at[2, group],
            mate(j), feat,
        )

    def spread_in(k):
        j = (group + k) % 8
        return remote(
            totals.at[group], totals.at[j], reduce_send.at[2, j], reduce_recv.at[2, j], mate(j),
            feat,
        )

    for k in range(1, 8):
        spread(k).start()
    for k in range(1, 8):
        spread_in(k).wait()
    done = totals[...].reshape(64, 384)
    gself_ref[...] = done[:, 0:128]
    gneigh_ref[...] = done[:, 128:256]
    gbias_ref[...] = done[:, 256:384].T[0:1, :]


def local(
    features, w_self, w_neigh, hidden_bias, cotangent, hub_local, send_rows, send_count,
    tile_values, tile_target, tile_anchor, tile_count,
):
    cols = features.shape[1]
    operands = (
        features, w_self, w_neigh, hidden_bias.reshape(1, -1), cotangent, hub_local, send_rows[0],
        send_count, tile_values, tile_target, tile_anchor, tile_count,
    )
    vmem = pl.BlockSpec(memory_space=pltpu.VMEM)
    scalars = (7, 11)
    hidden, grad_self, grad_neigh, bias_grad = pl.pallas_call(
        layer_kernel,
        name="layer",
        out_shape=(
            jax.ShapeDtypeStruct((64, cols), BF16),
            jax.ShapeDtypeStruct((64, 128), F32),
            jax.ShapeDtypeStruct((64, 128), F32),
            jax.ShapeDtypeStruct((1, 64), F32),
        ),
        in_specs=[pl.BlockSpec(memory_space=pl.ANY)] * 12,
        out_specs=(vmem,) * 4,
        scratch_shapes=[
            (pltpu.SMEM if i in scalars else pltpu.VMEM)(operand.shape, operand.dtype)
            for i, operand in enumerate(operands)
        ]
        + [
            pltpu.VMEM((112, 32, 128), BF16),
            pltpu.VMEM((NF, 32, cols), BF16),
            pltpu.VMEM((512, 256), BF16),
            pltpu.VMEM((NN, 32, 128), BF16),
            pltpu.VMEM((32, 128), BF16),
            pltpu.VMEM((32, 128), BF16),
            pltpu.VMEM((32, 128), BF16),
            pltpu.VMEM((32, 128), BF16),
            pltpu.VMEM((8, 384), I32),
            pltpu.SMEM((8, 384), I32),
            pltpu.VMEM((TILES, 32, 128), F32),
            pltpu.VMEM((NF, 32, cols), BF16),
            pltpu.VMEM((2, 64, 128), BF16),
            pltpu.VMEM((64, 128), F32),
            pltpu.VMEM((64, cols), F32),
            pltpu.VMEM((64, 384), F32),
            pltpu.VMEM((8, 8, 384), F32),
            pltpu.VMEM((8, 8, 384), F32),
            pltpu.VMEM((8, 384), F32),
            pltpu.VMEM((8, 8, 384), F32),
            pltpu.VMEM((8, 8, 384), F32),
            pltpu.SemaphoreType.DMA((12,)),
            pltpu.SemaphoreType.DMA,
            pltpu.SemaphoreType.DMA((NN,)),
            pltpu.SemaphoreType.DMA((NN,)),
            pltpu.SemaphoreType.DMA((NF,)),
            pltpu.SemaphoreType.DMA((NF,)),
            pltpu.SemaphoreType.DMA((8,)),
            pltpu.SemaphoreType.DMA((8,)),
            pltpu.SemaphoreType.DMA((3, PARTS)),
            pltpu.SemaphoreType.DMA((3, PARTS)),
            pltpu.SemaphoreType.DMA((3, 8)),
            pltpu.SemaphoreType.DMA((3, 8)),
        ],
        compiler_params=pltpu.CompilerParams(
            collective_id=0, has_side_effects=True, vmem_limit_bytes=56 * 2**20
        ),
    )(*operands)
    return hidden, grad_self.T, grad_neigh.T, bias_grad.reshape(-1)


def solution(mesh):
    in_specs = (
        P("feat", "nodes"), P(), P(), P(), P("feat", "nodes"), P("nodes", None),
        P("nodes", None, None), P("nodes", None), P("nodes", None, None), P("nodes", None),
        P("nodes", None), P("nodes"),
    )
    out_specs = (P("feat", "nodes"), P(None, "feat"), P(None, "feat"), P("feat"))
    return jax.shard_map(local, mesh=mesh, in_specs=in_specs, out_specs=out_specs, check_vma=False)
```

```python
import jax
import jax.numpy as jnp
from jax import lax
from jax.experimental import pallas as pl
from jax.experimental.pallas import tpu as pltpu
from jax.sharding import PartitionSpec as P

MESH = pl.DeviceIdType.MESH
NX, NZ, NN, NF = 4, 8, 64, 4
TILES = 352
BLOCKS = 32
UNROLL = 32
FLIPS = 16
FAR_FIRST = (4, 3, 5, 2, 6, 1, 7)
PARTS = 8
LAST = (((1,), (1,)), ((), ()))
F32 = jnp.float32
BF16 = jnp.bfloat16
I32 = jnp.int32


def peer_signal(barrier, node, part):
    pl.semaphore_signal(
        barrier, inc=1, device_id={"nodes": node, "feat": part}, device_id_type=MESH
    )


def remote(src, dst, send_sem, recv_sem, node, part):
    return pltpu.make_async_remote_copy(
        src_ref=src, dst_ref=dst, send_sem=send_sem, recv_sem=recv_sem,
        device_id={"nodes": node, "feat": part}, device_id_type=MESH,
    )


def started(copy):
    copy.start()
    return copy


def layer_kernel(
    feat_in, wself_in, wneigh_in, bias_in, cot_in, hub_in, rows_in, count_in, values_in, target_in,
    anchor_in, live_in, hidden_ref, gself_ref, gneigh_ref, gbias_ref,
    feat_ref, wself_ref, wneigh_ref, bias_ref, cot_ref, hub_ref, rows_ref, count_ref, values_ref,
    target_ref, anchor_ref, live_ref,
    src_ref, full_ref, stacked, outbox, hub0, hub0_in, hub_parts, table, order, running,
    aggs, weights, bias, own_term, sums, pieces, inbox, partial, crossbox, totals,
    load_sem, table_sem, halo_send, halo_recv, feat_send, feat_recv, hub_send, hub_recv,
    agg_send, agg_recv, reduce_send, reduce_recv,
):
    me = lax.axis_index("nodes")
    feat = lax.axis_index("feat")
    core = me % 2
    z = (me // 2) % NZ
    x = me // (2 * NZ)
    loads = [
        started(pltpu.make_async_copy(src, dst, load_sem.at[i]))
        for i, (src, dst) in enumerate(
            (
                (feat_in, feat_ref), (rows_in, rows_ref), (hub_in, hub_ref), (count_in, count_ref),
                (target_in, target_ref), (anchor_in, anchor_ref), (live_in, live_ref),
                (wself_in, wself_ref), (wneigh_in, wneigh_ref), (bias_in, bias_ref),
                (cot_in, cot_ref), (values_in, values_ref),
            )
        )
    ]
    barrier = pltpu.get_barrier_semaphore()

    def node_signal(k, _):
        peer_signal(barrier, (me + k) % NN, feat)
        return 0

    lax.fori_loop(1, NN, node_signal, 0)
    for k in range(1, NF):
        peer_signal(barrier, me, (feat + k) % NF)

    for copy in loads[:4]:
        copy.wait()
    for h in range(16):
        stacked[h * 32 : (h + 1) * 32, :] = feat_ref[:, h * 256 : (h + 1) * 256]
    lane = lax.broadcasted_iota(I32, (1, 128), 1)

    def pick(indices):
        down256 = lax.broadcasted_iota(I32, (256, 256), 0)
        hots = [(down256 == (index & 255)).astype(F32).astype(BF16) for index in indices]
        parts = [jnp.dot(stacked[...], hot, preferred_element_type=F32) for hot in hots]
        picked = []
        for index, part in zip(indices, parts):
            high = index >> 8
            out = jnp.zeros((32, 256), F32)
            for h in range(16):
                out = jnp.where(high == h, part[h * 32 : (h + 1) * 32], out)
            picked.append(out.astype(BF16))
        return picked

    def fill(chips):
        indices = []
        for chip in chips:
            pair = [
                jnp.where(lane < count_ref[0, node], rows_ref[pl.ds(node, 1), :], -1)
                for node in (2 * chip, 2 * chip + 1)
            ]
            indices.append(jnp.concatenate(pair, axis=1))
        for chip, rows in zip(chips, pick(indices)):
            outbox[2 * chip] = rows[:, :128]
            outbox[2 * chip + 1] = rows[:, 128:]

    def halo_copy(node):
        return remote(
            outbox.at[node], src_ref.at[32 + me], halo_send.at[node], halo_recv.at[me], node, feat
        )

    def chip_at(k, dz):
        dx = 2 + (1 - 2 * (k % 2)) * ((k + 1) // 2)
        return ((x + dx) % NX) * NZ + (z + dz) % NZ

    def send(chip):
        halo_copy(2 * chip).start()
        halo_copy(2 * chip + 1).start()

    def between(i, _):
        chips = [
            chip_at(2 * (i % 2) + j // 2, 4 + (2 * (j % 2) - 1) * (1 + i // 2)) for j in range(4)
        ]
        fill(chips)
        for chip in chips:
            send(chip)
        return 0

    sibling = me + 1 - 2 * core
    hubs = jnp.concatenate([hub_ref[...]] * 4, axis=1)
    hubs = jnp.where(lane // 32 % 2 == core, hubs, -1)
    own_hubs = pick([jnp.concatenate([hubs, jnp.full_like(hubs, -1)], axis=1)])[0][:, :128]
    hub0[...] = jnp.where(lane < 64, own_hubs[:16], own_hubs[16:])
    src_ref[32 + me] = jnp.zeros((32, 128), BF16)
    opposite = [chip_at(k, 4) for k in range(4)]
    fill(opposite)
    pl.semaphore_wait(barrier, NN - 1 + NF - 1)

    first = started(remote(hub0, hub0_in, hub_send.at[0], hub_recv.at[0], sibling, feat))
    feat_copies = [
        started(
            remote(
                feat_ref, full_ref.at[feat], feat_send.at[k], feat_recv.at[k], me,
                (feat + k) % NF,
            )
        )
        for k in range(1, NF)
    ]
    for chip in opposite:
        send(chip)
    lax.fori_loop(0, 1, between, 0)
    first.wait()
    hub_parts[x, z] = hub0[...] + hub0_in[...]

    def chip_hubs(k, zz):
        return remote(
            hub_parts.at[x, z], hub_parts.at[x, zz], hub_send.at[k], hub_recv.at[k],
            x * 2 * NZ + ((z + k) % NZ) * 2 + core, feat,
        )

    for k in FAR_FIRST:
        chip_hubs(k, z).start()
    lax.fori_loop(1, 6, between, 0)
    level = [chip_at(k, 0) for k in range(3)] + [me // 2]
    fill(level)
    for chip in level[:3]:
        send(chip)
    halo_copy(sibling).start()

    for copy in loads[4:-1]:
        copy.wait()
    down = lax.broadcasted_iota(I32, (TILES, TILES), 0)
    along = lax.broadcasted_iota(I32, (TILES, TILES), 1)
    slot_row = lax.broadcasted_iota(I32, (1, TILES), 1)
    key_row = jnp.where(slot_row < live_ref[0], jnp.clip(target_ref[...], 0, BLOCKS - 1), BLOCKS)
    anchor_row = jnp.clip(anchor_ref[...], 0, 111)

    def column(row):
        return jnp.sum(jnp.where(down == along, row, 0), axis=1, keepdims=True)

    key = column(key_row)
    ahead = (key_row < key) | ((key_row == key) & (along < down))
    rank = jnp.sum(jnp.where(ahead, 1, 0), axis=1, keepdims=True)
    placed = rank == along

    def sorted_row(col):
        return jnp.sum(jnp.where(placed, col, 0), axis=0, keepdims=True)

    key_sorted = sorted_row(key)
    slot_col = lax.broadcasted_iota(I32, (TILES, 1), 0)
    table[0:1, 0:TILES] = sorted_row(slot_col)
    table[1:2, 0:TILES] = sorted_row(column(anchor_row))
    table[2:3, 0:TILES] = key_sorted
    blocks_along = lax.broadcasted_iota(I32, (TILES, 128), 1)
    table[3:4, 0:128] = jnp.maximum(
        jnp.sum(jnp.where(key <= blocks_along, 1, 0), axis=0, keepdims=True) - 1, 0
    )
    to_scalars = started(pltpu.make_async_copy(table, order, table_sem))

    for k in range(1, NZ):
        chip_hubs(k, (z - k) % NZ).wait()

    def row_hubs(k, xx):
        return remote(
            hub_parts.at[x], hub_parts.at[xx], hub_send.at[7 + k], hub_recv.at[7 + k],
            ((x + k) % NX) * 2 * NZ + z * 2 + core, feat,
        )

    for k in (2, 1, 3):
        row_hubs(k, x).start()

    def mine(ref):
        part = ref[:, 0:64]
        for k in range(1, NF):
            part = jnp.where(feat == k, ref[:, k * 64 : (k + 1) * 64], part)
        return part

    weights[0] = mine(wself_ref).T
    weights[1] = mine(wneigh_ref).T
    bias[...] = jnp.broadcast_to(mine(bias_ref), (128, 64)).T
    sums[...] = jnp.zeros_like(sums)
    for b in range(32):
        src_ref[b] = feat_ref[:, b * 128 : (b + 1) * 128]
    full_ref[feat] = feat_ref[...]
    to_scalars.wait()
    loads[-1].wait()

    def flip(b, _):
        tiles = [values_ref[b * FLIPS + j].T for j in range(FLIPS)]
        for j in range(FLIPS):
            values_ref[b * FLIPS + j] = tiles[j]
        return 0

    lax.fori_loop(0, TILES // FLIPS, flip, 0)
    for k in range(1, NX):
        row_hubs(k, (x - k) % NX).wait()
    for b in range(16):
        even = hub_parts[b // 4, 2 * (b % 4)]
        odd = hub_parts[b // 4, 2 * (b % 4) + 1]
        src_ref[96 + b, 0:16, :] = jnp.concatenate([even[:, :64], odd[:, :64]], axis=1)
        src_ref[96 + b, 16:32, :] = jnp.concatenate([even[:, 64:], odd[:, 64:]], axis=1)

    def arrived(k, _):
        node = (me + k) % NN
        remote(
            outbox.at[node], src_ref.at[32 + node], halo_send.at[node], halo_recv.at[node], node,
            feat,
        ).wait()
        return 0

    lax.fori_loop(1, NN, arrived, 0)

    empty = jnp.zeros((32, 128), BF16)

    def batch(b, total):
        products = []
        for j in range(0, UNROLL, 2):
            slot = b * UNROLL + j
            one = src_ref[order[1, slot]]
            two = src_ref[order[1, slot + 1]]
            rows = jnp.concatenate(
                [jnp.concatenate([one, empty], axis=1), jnp.concatenate([empty, two], axis=1)],
                axis=0,
            )
            pair = jnp.concatenate(
                [values_ref[order[0, slot]], values_ref[order[0, slot + 1]]], axis=0
            )
            product = jnp.dot(rows, pair, preferred_element_type=F32)
            products += [product[:32], product[32:]]
        for j in range(UNROLL):
            slot = b * UNROLL + j
            same = order[2, slot] == order[2, jnp.maximum(slot - 1, 0)]
            total = jnp.where(same, total, 0.0) + products[j]
            running[slot] = total
        return total

    lax.fori_loop(0, TILES // UNROLL, batch, jnp.zeros((32, 128), F32))

    width = cot_ref.shape[1] // PARTS

    def at(c):
        return pl.ds(pl.multiple_of(c * width, width), width)

    def direct(c, way):
        slot = (1 - way) // 2
        own = aggs.at[c, feat]
        return remote(
            own, own, agg_send.at[slot, c], agg_recv.at[slot, c], me, (feat + way) % NF
        )

    def relay(c):
        way = 1 - 2 * (c % 2)
        theirs = aggs.at[c, (feat - way) % NF]
        return remote(
            theirs, theirs, agg_send.at[2, c], agg_recv.at[2, c], me, (feat + way) % NF
        )

    def give(c, _):
        ends = [running[order[3, c * 4 + k]].astype(BF16) for k in range(4)]
        aggs[c, feat] = jnp.concatenate(ends, axis=1)
        direct(c, 1).start()
        direct(c, -1).start()
        return 0

    lax.fori_loop(0, PARTS, give, 0)
    for copy in feat_copies:
        copy.wait()

    def own_part(c, _):
        own = full_ref[:, :, at(c)].reshape(128, width)
        own_term[:, at(c)] = (
            jnp.dot(weights[0], own, preferred_element_type=F32) + bias[:, 0:1]
        )
        return 0

    def columns(c):
        span = at(c)
        relay(c).wait()
        own = full_ref[:, :, span].reshape(128, width)
        neigh = aggs[c].reshape(128, width)
        pre = own_term[:, span] + jnp.dot(weights[1], neigh, preferred_element_type=F32)
        gate = jax.nn.sigmoid(pre)
        hidden_ref[:, span] = (pre * gate).astype(BF16)
        grad = (cot_ref[:, span].astype(F32) * gate * (1.0 + pre * (1.0 - gate))).astype(BF16)
        every = jnp.concatenate([own, neigh, jnp.ones((128, width), BF16)], axis=0)
        sums[...] += lax.dot_general(grad, every, LAST, preferred_element_type=F32)

    def pass_on(c, _):
        direct(c, 1).wait()
        direct(c, -1).wait()
        relay(c).start()
        return 0

    def turn(c, _):
        columns(c)
        return 0

    lax.fori_loop(0, PARTS, own_part, 0)
    lax.fori_loop(0, PARTS, pass_on, 0)
    lax.fori_loop(0, PARTS, turn, 0)

    group = x * 2 + core

    def mate(j):
        return (j // 2) * 2 * NZ + z * 2 + j % 2

    def across(zz):
        return x * 2 * NZ + zz * 2 + core

    for j in range(8):
        pieces[j] = sums[8 * j : 8 * j + 8, :]
    own_piece = pieces.at[group]

    def scatter(k):
        j = (group + k) % 8
        return remote(
            pieces.at[j], inbox.at[group], reduce_send.at[0, j], reduce_recv.at[0, group],
            mate(j), feat,
        )

    def scatter_in(k):
        j = (group + k) % 8
        return remote(
            pieces.at[j], inbox.at[j], reduce_send.at[0, j], reduce_recv.at[0, j], mate(j), feat
        )

    for k in FAR_FIRST:
        scatter(k).start()
    inbox[group] = own_piece[...]
    for k in range(1, 8):
        scatter_in(k).wait()
    crossed = inbox[0]
    for j in range(1, 8):
        crossed = crossed + inbox[j]
    partial[...] = crossed
    crossbox[z] = crossed

    def cross(k):
        zz = (z + k) % NZ
        return remote(
            partial, crossbox.at[z], reduce_send.at[1, zz], reduce_recv.at[1, z], across(zz), feat
        )

    def cross_in(k):
        zz = (z + k) % NZ
        return remote(
            partial, crossbox.at[zz], reduce_send.at[1, zz], reduce_recv.at[1, zz], across(zz),
            feat,
        )

    for k in FAR_FIRST:
        cross(k).start()
    for k in range(1, 8):
        cross_in(k).wait()
    total = crossbox[0]
    for j in range(1, 8):
        total = total + crossbox[j]
    totals[group] = total

    def spread(k):
        j = (group + k) % 8
        return remote(
            totals.at[group], totals.at[group], reduce_send.at[2, j], reduce_recv.at[2, group],
            mate(j), feat,
        )

    def spread_in(k):
        j = (group + k) % 8
        return remote(
            totals.at[group], totals.at[j], reduce_send.at[2, j], reduce_recv.at[2, j], mate(j),
            feat,
        )

    for k in FAR_FIRST:
        spread(k).start()
    for k in range(1, 8):
        spread_in(k).wait()
    done = totals[...].reshape(64, 384)
    gself_ref[...] = done[:, 0:128]
    gneigh_ref[...] = done[:, 128:256]
    gbias_ref[...] = done[:, 256:384].T[0:1, :]


def local(
    features, w_self, w_neigh, hidden_bias, cotangent, hub_local, send_rows, send_count,
    tile_values, tile_target, tile_anchor, tile_count,
):
    cols = features.shape[1]
    operands = (
        features, w_self, w_neigh, hidden_bias.reshape(1, -1), cotangent, hub_local, send_rows[0],
        send_count, tile_values, tile_target, tile_anchor,
    )
    operands = tuple(
        pltpu.with_memory_space_constraint(operand, pltpu.MemorySpace.HBM) for operand in operands
    ) + (tile_count,)
    vmem = pl.BlockSpec(memory_space=pltpu.VMEM)
    scalars = (7, 11)
    hidden, grad_self, grad_neigh, bias_grad = pl.pallas_call(
        layer_kernel,
        name="layer",
        out_shape=(
            jax.ShapeDtypeStruct((64, cols), BF16),
            jax.ShapeDtypeStruct((64, 128), F32),
            jax.ShapeDtypeStruct((64, 128), F32),
            jax.ShapeDtypeStruct((1, 64), F32),
        ),
        in_specs=[pl.BlockSpec(memory_space=pl.ANY)] * 12,
        out_specs=(vmem,) * 4,
        scratch_shapes=[
            (pltpu.SMEM if i in scalars else pltpu.VMEM)(operand.shape, operand.dtype)
            for i, operand in enumerate(operands)
        ]
        + [
            pltpu.VMEM((112, 32, 128), BF16),
            pltpu.VMEM((NF, 32, cols), BF16),
            pltpu.VMEM((512, 256), BF16),
            pltpu.VMEM((NN, 32, 128), BF16),
            pltpu.VMEM((16, 128), BF16),
            pltpu.VMEM((16, 128), BF16),
            pltpu.VMEM((NX, NZ, 16, 128), BF16),
            pltpu.VMEM((8, 384), I32),
            pltpu.SMEM((8, 384), I32),
            pltpu.VMEM((TILES, 32, 128), F32),
            pltpu.VMEM((PARTS, NF, 32, cols // PARTS), BF16),
            pltpu.VMEM((2, 64, 128), BF16),
            pltpu.VMEM((64, 128), F32),
            pltpu.VMEM((64, cols), F32),
            pltpu.VMEM((64, 384), F32),
            pltpu.VMEM((8, 8, 384), F32),
            pltpu.VMEM((8, 8, 384), F32),
            pltpu.VMEM((8, 384), F32),
            pltpu.VMEM((8, 8, 384), F32),
            pltpu.VMEM((8, 8, 384), F32),
            pltpu.SemaphoreType.DMA((12,)),
            pltpu.SemaphoreType.DMA,
            pltpu.SemaphoreType.DMA((NN,)),
            pltpu.SemaphoreType.DMA((NN,)),
            pltpu.SemaphoreType.DMA((NF,)),
            pltpu.SemaphoreType.DMA((NF,)),
            pltpu.SemaphoreType.DMA((11,)),
            pltpu.SemaphoreType.DMA((11,)),
            pltpu.SemaphoreType.DMA((3, PARTS)),
            pltpu.SemaphoreType.DMA((3, PARTS)),
            pltpu.SemaphoreType.DMA((3, 8)),
            pltpu.SemaphoreType.DMA((3, 8)),
        ],
        compiler_params=pltpu.CompilerParams(
            collective_id=0, has_side_effects=True, vmem_limit_bytes=40 * 2**20
        ),
    )(*operands)
    return hidden, grad_self.T, grad_neigh.T, bias_grad.reshape(-1)


def solution(mesh):
    in_specs = (
        P("feat", "nodes"), P(), P(), P(), P("feat", "nodes"), P("nodes", None),
        P("nodes", None, None), P("nodes", None), P("nodes", None, None), P("nodes", None),
        P("nodes", None), P("nodes"),
    )
    out_specs = (P("feat", "nodes"), P(None, "feat"), P(None, "feat"), P("feat"))
    return jax.shard_map(local, mesh=mesh, in_specs=in_specs, out_specs=out_specs, check_vma=False)
```

```python
import jax
import jax.numpy as jnp
from jax import lax
from jax.experimental import pallas as pl
from jax.experimental.pallas import tpu as pltpu
from jax.sharding import PartitionSpec as P

MESH = pl.DeviceIdType.MESH
NX, NZ, NN, NF = 4, 8, 64, 4
TILES = 352
BLOCKS = 32
UNROLL = 32
FLIPS = 16
FAR_FIRST = (4, 3, 5, 2, 6, 1, 7)
PARTS = 8
RELAYED = 6
LAST = (((1,), (1,)), ((), ()))
F32 = jnp.float32
BF16 = jnp.bfloat16
I32 = jnp.int32


def peer_signal(barrier, node, part):
    pl.semaphore_signal(
        barrier, inc=1, device_id={"nodes": node, "feat": part}, device_id_type=MESH
    )


def remote(src, dst, send_sem, recv_sem, node, part):
    return pltpu.make_async_remote_copy(
        src_ref=src, dst_ref=dst, send_sem=send_sem, recv_sem=recv_sem,
        device_id={"nodes": node, "feat": part}, device_id_type=MESH,
    )


def started(copy):
    copy.start()
    return copy


def layer_kernel(
    feat_in, wself_in, wneigh_in, bias_in, cot_in, hub_in, rows_in, count_in, values_in, target_in,
    anchor_in, live_in, hidden_ref, grads_ref,
    feat_ref, wself_ref, wneigh_ref, bias_ref, cot_ref, hub_ref, rows_ref, count_ref, values_ref,
    target_ref, anchor_ref, live_ref,
    src_ref, full_ref, stacked, outbox, hub0, hub0_in, hub_parts, table, order, running,
    aggs, weights, bias, own_term, sums, pieces, inbox, partial, crossbox, totals,
    load_sem, table_sem, halo_send, halo_recv, feat_send, feat_recv, hub_send, hub_recv,
    agg_send, agg_recv, reduce_send, reduce_recv,
):
    me = lax.axis_index("nodes")
    feat = lax.axis_index("feat")
    core = me % 2
    z = (me // 2) % NZ
    x = me // (2 * NZ)
    loads = [
        started(pltpu.make_async_copy(src, dst, load_sem.at[i]))
        for i, (src, dst) in enumerate(
            (
                (feat_in, feat_ref), (rows_in, rows_ref), (hub_in, hub_ref), (count_in, count_ref),
                (target_in, target_ref), (anchor_in, anchor_ref), (live_in, live_ref),
                (wself_in, wself_ref), (wneigh_in, wneigh_ref), (bias_in, bias_ref),
                (cot_in, cot_ref), (values_in, values_ref),
            )
        )
    ]
    barrier = pltpu.get_barrier_semaphore()

    def node_signal(k, _):
        peer_signal(barrier, (me + k) % NN, feat)
        return 0

    lax.fori_loop(1, NN, node_signal, 0)
    for k in range(1, NF):
        peer_signal(barrier, me, (feat + k) % NF)

    for copy in loads[:4]:
        copy.wait()
    for h in range(16):
        stacked[h * 32 : (h + 1) * 32, :] = feat_ref[:, h * 256 : (h + 1) * 256]
    lane = lax.broadcasted_iota(I32, (1, 128), 1)

    def pick(indices):
        down256 = lax.broadcasted_iota(I32, (256, 256), 0)
        hots = [(down256 == (index & 255)).astype(F32).astype(BF16) for index in indices]
        parts = [jnp.dot(stacked[...], hot, preferred_element_type=F32) for hot in hots]
        picked = []
        for index, part in zip(indices, parts):
            high = index >> 8
            out = jnp.zeros((32, 256), F32)
            for h in range(16):
                out = jnp.where(high == h, part[h * 32 : (h + 1) * 32], out)
            picked.append(out.astype(BF16))
        return picked

    def fill(chips):
        indices = []
        for chip in chips:
            pair = [
                jnp.where(lane < count_ref[0, node], rows_ref[pl.ds(node, 1), :], -1)
                for node in (2 * chip, 2 * chip + 1)
            ]
            indices.append(jnp.concatenate(pair, axis=1))
        for chip, rows in zip(chips, pick(indices)):
            outbox[2 * chip] = rows[:, :128]
            outbox[2 * chip + 1] = rows[:, 128:]

    def halo_copy(node):
        return remote(
            outbox.at[node], src_ref.at[32 + me], halo_send.at[node], halo_recv.at[me], node, feat
        )

    def chip_at(k, dz):
        dx = 2 + (1 - 2 * (k % 2)) * ((k + 1) // 2)
        return ((x + dx) % NX) * NZ + (z + dz) % NZ

    def send(chip):
        halo_copy(2 * chip).start()
        halo_copy(2 * chip + 1).start()

    def between_chips(i):
        return [
            chip_at(2 * (i % 2) + j // 2, 4 + (2 * (j % 2) - 1) * (1 + i // 2)) for j in range(4)
        ]

    def between(i, _):
        chips = between_chips(i)
        fill(chips)
        for chip in chips:
            send(chip)
        return 0

    sibling = me + 1 - 2 * core
    hubs = jnp.concatenate([hub_ref[...]] * 4, axis=1)
    hubs = jnp.where(lane // 32 % 2 == core, hubs, -1)
    own_hubs = pick([jnp.concatenate([hubs, jnp.full_like(hubs, -1)], axis=1)])[0][:, :128]
    hub0[...] = jnp.where(lane < 64, own_hubs[:16], own_hubs[16:])
    src_ref[32 + me] = jnp.zeros((32, 128), BF16)
    opposite = [chip_at(k, 4) for k in range(4)]
    fill(opposite)
    pl.semaphore_wait(barrier, NN - 1 + NF - 1)

    first = started(remote(hub0, hub0_in, hub_send.at[0], hub_recv.at[0], sibling, feat))
    feat_copies = [
        started(
            remote(
                feat_ref, full_ref.at[feat], feat_send.at[k], feat_recv.at[k], me,
                (feat + k) % NF,
            )
        )
        for k in range(1, NF)
    ]
    for chip in opposite:
        send(chip)
    lax.fori_loop(0, 1, between, 0)
    first.wait()
    hub_parts[x, z] = hub0[...] + hub0_in[...]

    def chip_hubs(k, zz):
        return remote(
            hub_parts.at[x, z], hub_parts.at[x, zz], hub_send.at[k], hub_recv.at[k],
            x * 2 * NZ + ((z + k) % NZ) * 2 + core, feat,
        )

    for k in FAR_FIRST:
        chip_hubs(k, z).start()
    lax.fori_loop(1, 6, between, 0)
    level = [chip_at(k, 0) for k in range(3)] + [me // 2]
    fill(level)
    for chip in level[:3]:
        send(chip)
    halo_copy(sibling).start()

    for copy in loads[4:-1]:
        copy.wait()
    down = lax.broadcasted_iota(I32, (TILES, TILES), 0)
    along = lax.broadcasted_iota(I32, (TILES, TILES), 1)
    slot_row = lax.broadcasted_iota(I32, (1, TILES), 1)
    key_row = jnp.where(slot_row < live_ref[0], jnp.clip(target_ref[...], 0, BLOCKS - 1), BLOCKS)
    anchor_row = jnp.clip(anchor_ref[...], 0, 111)

    def column(row):
        return jnp.sum(jnp.where(down == along, row, 0), axis=1, keepdims=True)

    key = column(key_row)
    ahead = (key_row < key) | ((key_row == key) & (along < down))
    rank = jnp.sum(jnp.where(ahead, 1, 0), axis=1, keepdims=True)
    placed = rank == along

    def sorted_row(col):
        return jnp.sum(jnp.where(placed, col, 0), axis=0, keepdims=True)

    key_sorted = sorted_row(key)
    slot_col = lax.broadcasted_iota(I32, (TILES, 1), 0)
    table[0:1, 0:TILES] = sorted_row(slot_col)
    table[1:2, 0:TILES] = sorted_row(column(anchor_row))
    table[2:3, 0:TILES] = key_sorted
    blocks_along = lax.broadcasted_iota(I32, (TILES, 128), 1)
    table[3:4, 0:128] = jnp.maximum(
        jnp.sum(jnp.where(key <= blocks_along, 1, 0), axis=0, keepdims=True) - 1, 0
    )
    to_scalars = started(pltpu.make_async_copy(table, order, table_sem))

    for k in range(1, NZ):
        chip_hubs(k, (z - k) % NZ).wait()

    def row_hubs(k, xx):
        return remote(
            hub_parts.at[x], hub_parts.at[xx], hub_send.at[7 + k], hub_recv.at[7 + k],
            ((x + k) % NX) * 2 * NZ + z * 2 + core, feat,
        )

    for k in (2, 1, 3):
        row_hubs(k, x).start()

    def mine(ref):
        part = ref[:, 0:64]
        for k in range(1, NF):
            part = jnp.where(feat == k, ref[:, k * 64 : (k + 1) * 64], part)
        return part

    weights[0] = mine(wself_ref).T
    weights[1] = mine(wneigh_ref).T
    bias[...] = jnp.broadcast_to(mine(bias_ref), (128, 64)).T
    sums[...] = jnp.zeros_like(sums)
    for b in range(32):
        src_ref[b] = feat_ref[:, b * 128 : (b + 1) * 128]
    full_ref[feat] = feat_ref[...]
    to_scalars.wait()
    loads[-1].wait()

    def flip(b, _):
        tiles = [values_ref[b * FLIPS + j].T for j in range(FLIPS)]
        for j in range(FLIPS):
            values_ref[b * FLIPS + j] = tiles[j]
        return 0

    lax.fori_loop(0, TILES // FLIPS, flip, 0)
    for k in range(1, NX):
        row_hubs(k, (x - k) % NX).wait()
    for b in range(16):
        even = hub_parts[b // 4, 2 * (b % 4)]
        odd = hub_parts[b // 4, 2 * (b % 4) + 1]
        src_ref[96 + b, 0:16, :] = jnp.concatenate([even[:, :64], odd[:, :64]], axis=1)
        src_ref[96 + b, 16:32, :] = jnp.concatenate([even[:, 64:], odd[:, 64:]], axis=1)

    def arrived(node):
        remote(
            outbox.at[node], src_ref.at[32 + node], halo_send.at[node], halo_recv.at[node], node,
            feat,
        ).wait_recv()

    def between_arrived(i, _):
        for chip in between_chips(i):
            arrived(2 * chip)
            arrived(2 * chip + 1)
        return 0

    for chip in opposite:
        arrived(2 * chip)
        arrived(2 * chip + 1)
    lax.fori_loop(0, 6, between_arrived, 0)
    for chip in level[:3]:
        arrived(2 * chip)
        arrived(2 * chip + 1)
    arrived(sibling)

    empty = jnp.zeros((32, 128), BF16)

    def batch(b, total):
        products = []
        for j in range(0, UNROLL, 2):
            slot = b * UNROLL + j
            one = src_ref[order[1, slot]]
            two = src_ref[order[1, slot + 1]]
            rows = jnp.concatenate(
                [jnp.concatenate([one, empty], axis=1), jnp.concatenate([empty, two], axis=1)],
                axis=0,
            )
            pair = jnp.concatenate(
                [values_ref[order[0, slot]], values_ref[order[0, slot + 1]]], axis=0
            )
            product = jnp.dot(rows, pair, preferred_element_type=F32)
            products += [product[:32], product[32:]]
        for j in range(UNROLL):
            slot = b * UNROLL + j
            same = order[2, slot] == order[2, jnp.maximum(slot - 1, 0)]
            total = jnp.where(same, total, 0.0) + products[j]
            running[slot] = total
        return total

    lax.fori_loop(0, TILES // UNROLL, batch, jnp.zeros((32, 128), F32))

    width = cot_ref.shape[1] // PARTS

    def at(c):
        return pl.ds(pl.multiple_of(c * width, width), width)

    def direct(c, way):
        slot = (1 - way) // 2
        own = aggs.at[c, feat]
        return remote(
            own, own, agg_send.at[slot, c], agg_recv.at[slot, c], me, (feat + way) % NF
        )

    def relay(c):
        way = 1 - 2 * (c % 2)
        theirs = aggs.at[c, (feat - way) % NF]
        return remote(
            theirs, theirs, agg_send.at[2, c], agg_recv.at[2, c], me, (feat + way) % NF
        )

    def over(c):
        own = aggs.at[c, feat]
        return remote(own, own, agg_send.at[2, c], agg_recv.at[2, c], me, (feat + 2) % NF)

    def give(c, _):
        ends = [running[order[3, c * 4 + k]].astype(BF16) for k in range(4)]
        aggs[c, feat] = jnp.concatenate(ends, axis=1)

        return 0

    def give_all(c, _):
        give(c, 0)
        over(c).start()
        direct(c, 1).start()
        direct(c, -1).start()
        return 0

    def give_near(c, _):
        give(c, 0)
        direct(c, 1).start()
        direct(c, -1).start()
        return 0

    lax.fori_loop(RELAYED, PARTS, give_all, 0)
    lax.fori_loop(0, RELAYED, give_near, 0)

    def halo_left(k, _):
        halo_copy((me + k) % NN).wait_send()
        return 0

    lax.fori_loop(1, NN, halo_left, 0)
    for copy in feat_copies:
        copy.wait()

    def own_part(c, _):
        own = full_ref[:, :, at(c)].reshape(128, width)
        own_term[:, at(c)] = (
            jnp.dot(weights[0], own, preferred_element_type=F32) + bias[:, 0:1]
        )
        return 0

    def columns(c):
        span = at(c)
        relay(c).wait_recv()
        own = full_ref[:, :, span].reshape(128, width)
        neigh = aggs[c].reshape(128, width)
        pre = own_term[:, span] + jnp.dot(weights[1], neigh, preferred_element_type=F32)
        gate = jax.nn.sigmoid(pre)
        hidden_ref[:, span] = (pre * gate).astype(BF16)
        grad = (cot_ref[:, span].astype(F32) * gate * (1.0 + pre * (1.0 - gate))).astype(BF16)
        every = jnp.concatenate([own, neigh, jnp.ones((128, width), BF16)], axis=0)
        sums[...] += lax.dot_general(grad, every, LAST, preferred_element_type=F32)

    def pass_on(c, _):
        direct(c, 1).wait_recv()
        direct(c, -1).wait_recv()
        relay(c).start()
        return 0

    def final(c, _):
        columns(c)
        return 0

    def drain(c, _):
        direct(c, 1).wait_send()
        direct(c, -1).wait_send()
        relay(c).wait_send()
        return 0

    lax.fori_loop(0, PARTS, own_part, 0)
    lax.fori_loop(0, RELAYED, pass_on, 0)
    for c in range(RELAYED, PARTS):
        direct(c, 1).wait_recv()
        direct(c, -1).wait_recv()
    lax.fori_loop(RELAYED, PARTS, final, 0)
    lax.fori_loop(0, RELAYED, final, 0)

    group = x * 2 + core

    def mate(j):
        return (j // 2) * 2 * NZ + z * 2 + j % 2

    def across(zz):
        return x * 2 * NZ + zz * 2 + core

    for j in range(8):
        pieces[j] = sums[8 * j : 8 * j + 8, :]
    own_piece = pieces.at[group]

    def scatter(k):
        j = (group + k) % 8
        return remote(
            pieces.at[j], inbox.at[group], reduce_send.at[0, j], reduce_recv.at[0, group],
            mate(j), feat,
        )

    def scatter_in(k):
        j = (group + k) % 8
        return remote(
            pieces.at[j], inbox.at[j], reduce_send.at[0, j], reduce_recv.at[0, j], mate(j), feat
        )

    for k in FAR_FIRST:
        scatter(k).start()
    inbox[group] = own_piece[...]
    lax.fori_loop(0, PARTS, drain, 0)
    for k in range(1, 8):
        scatter_in(k).wait()
    crossed = inbox[0]
    for j in range(1, 8):
        crossed = crossed + inbox[j]
    partial[...] = crossed
    crossbox[z] = crossed

    def cross(k):
        zz = (z + k) % NZ
        return remote(
            partial, crossbox.at[z], reduce_send.at[1, zz], reduce_recv.at[1, z], across(zz), feat
        )

    def cross_in(k):
        zz = (z + k) % NZ
        return remote(
            partial, crossbox.at[zz], reduce_send.at[1, zz], reduce_recv.at[1, zz], across(zz),
            feat,
        )

    for k in FAR_FIRST:
        cross(k).start()
    for k in range(1, 8):
        cross_in(k).wait()
    total = crossbox[0]
    for j in range(1, 8):
        total = total + crossbox[j]
    totals[group] = total

    def spread(k):
        j = (group + k) % 8
        return remote(
            totals.at[group], totals.at[group], reduce_send.at[2, j], reduce_recv.at[2, group],
            mate(j), feat,
        )

    def spread_in(k):
        j = (group + k) % 8
        return remote(
            totals.at[group], totals.at[j], reduce_send.at[2, j], reduce_recv.at[2, j], mate(j),
            feat,
        )

    for k in FAR_FIRST:
        spread(k).start()
    for k in range(1, 8):
        spread_in(k).wait()
    grads_ref[...] = totals[...].reshape(64, 384)


def finish_kernel(hidden_ref, grads_ref, hidden_out, gself_out, gneigh_out, gbias_out, bias, sem):
    copies = [
        started(pltpu.make_async_copy(src, dst, sem.at[i]))
        for i, (src, dst) in enumerate(
            (
                (hidden_ref, hidden_out), (grads_ref.at[:, 0:128], gself_out),
                (grads_ref.at[:, 128:256], gneigh_out),
            )
        )
    ]
    bias[...] = grads_ref[:, 256:384].T[0:1, :]
    copies.append(started(pltpu.make_async_copy(bias, gbias_out, sem.at[3])))
    for copy in copies:
        copy.wait()


def local(
    features, w_self, w_neigh, hidden_bias, cotangent, hub_local, send_rows, send_count,
    tile_values, tile_target, tile_anchor, tile_count,
):
    cols = features.shape[1]
    operands = (
        features, w_self, w_neigh, hidden_bias.reshape(1, -1), cotangent, hub_local, send_rows[0],
        send_count, tile_values, tile_target, tile_anchor,
    )
    operands = tuple(
        pltpu.with_memory_space_constraint(operand, pltpu.MemorySpace.HBM) for operand in operands
    ) + (tile_count,)
    vmem = pl.BlockSpec(memory_space=pltpu.VMEM)
    scalars = (7, 11)
    hidden, grads = pl.pallas_call(
        layer_kernel,
        name="layer",
        out_shape=(
            jax.ShapeDtypeStruct((64, cols), BF16),
            jax.ShapeDtypeStruct((64, 384), F32),
        ),
        in_specs=[pl.BlockSpec(memory_space=pl.ANY)] * 12,
        out_specs=(vmem,) * 2,
        scratch_shapes=[
            (pltpu.SMEM if i in scalars else pltpu.VMEM)(operand.shape, operand.dtype)
            for i, operand in enumerate(operands)
        ]
        + [
            pltpu.VMEM((112, 32, 128), BF16),
            pltpu.VMEM((NF, 32, cols), BF16),
            pltpu.VMEM((512, 256), BF16),
            pltpu.VMEM((NN, 32, 128), BF16),
            pltpu.VMEM((16, 128), BF16),
            pltpu.VMEM((16, 128), BF16),
            pltpu.VMEM((NX, NZ, 16, 128), BF16),
            pltpu.VMEM((8, 384), I32),
            pltpu.SMEM((8, 384), I32),
            pltpu.VMEM((TILES, 32, 128), F32),
            pltpu.VMEM((PARTS, NF, 32, cols // PARTS), BF16),
            pltpu.VMEM((2, 64, 128), BF16),
            pltpu.VMEM((64, 128), F32),
            pltpu.VMEM((64, cols), F32),
            pltpu.VMEM((64, 384), F32),
            pltpu.VMEM((8, 8, 384), F32),
            pltpu.VMEM((8, 8, 384), F32),
            pltpu.VMEM((8, 384), F32),
            pltpu.VMEM((8, 8, 384), F32),
            pltpu.VMEM((8, 8, 384), F32),
            pltpu.SemaphoreType.DMA((12,)),
            pltpu.SemaphoreType.DMA,
            pltpu.SemaphoreType.DMA((NN,)),
            pltpu.SemaphoreType.DMA((NN,)),
            pltpu.SemaphoreType.DMA((NF,)),
            pltpu.SemaphoreType.DMA((NF,)),
            pltpu.SemaphoreType.DMA((11,)),
            pltpu.SemaphoreType.DMA((11,)),
            pltpu.SemaphoreType.DMA((3, PARTS)),
            pltpu.SemaphoreType.DMA((3, PARTS)),
            pltpu.SemaphoreType.DMA((3, 8)),
            pltpu.SemaphoreType.DMA((3, 8)),
        ],
        compiler_params=pltpu.CompilerParams(
            collective_id=0, has_side_effects=True, vmem_limit_bytes=40 * 2**20
        ),
    )(*operands)
    hidden, grad_self, grad_neigh, bias_grad = pl.pallas_call(
        finish_kernel,
        name="finish",
        out_shape=(
            jax.ShapeDtypeStruct((64, cols), BF16),
            jax.ShapeDtypeStruct((64, 128), F32),
            jax.ShapeDtypeStruct((64, 128), F32),
            jax.ShapeDtypeStruct((1, 64), F32),
        ),
        in_specs=[vmem] * 2,
        out_specs=(pl.BlockSpec(memory_space=pl.ANY),) * 4,
        scratch_shapes=[pltpu.VMEM((1, 64), F32), pltpu.SemaphoreType.DMA((4,))],
        compiler_params=pltpu.CompilerParams(vmem_limit_bytes=4 * 2**20),
    )(hidden, grads)
    return hidden, grad_self.T, grad_neigh.T, bias_grad.reshape(-1)


def solution(mesh):
    in_specs = (
        P("feat", "nodes"), P(), P(), P(), P("feat", "nodes"), P("nodes", None),
        P("nodes", None, None), P("nodes", None), P("nodes", None, None), P("nodes", None),
        P("nodes", None), P("nodes"),
    )
    out_specs = (P("feat", "nodes"), P(None, "feat"), P(None, "feat"), P("feat"))
    return jax.shard_map(local, mesh=mesh, in_specs=in_specs, out_specs=out_specs, check_vma=False)
```

```python
import jax
import jax.numpy as jnp
from jax import lax
from jax.experimental import pallas as pl
from jax.experimental.pallas import tpu as pltpu
from jax.sharding import PartitionSpec as P

MESH = pl.DeviceIdType.MESH
NX, NZ, NN, NF = 4, 8, 64, 4
TILES = 352
BLOCKS = 32
UNROLL = 88
FLIPS = 16
FAR_FIRST = (4, 3, 5, 2, 6, 1, 7)
PARTS = 8
RELAYED = 6
LAST = (((1,), (1,)), ((), ()))
F32 = jnp.float32
BF16 = jnp.bfloat16
I32 = jnp.int32


def peer_signal(barrier, node, part):
    pl.semaphore_signal(
        barrier, inc=1, device_id={"nodes": node, "feat": part}, device_id_type=MESH
    )


def remote(src, dst, send_sem, recv_sem, node, part):
    return pltpu.make_async_remote_copy(
        src_ref=src, dst_ref=dst, send_sem=send_sem, recv_sem=recv_sem,
        device_id={"nodes": node, "feat": part}, device_id_type=MESH,
    )


def started(copy):
    copy.start()
    return copy


def layer_kernel(
    feat_in, wself_in, wneigh_in, bias_in, cot_in, hub_in, rows_in, count_in, values_in, target_in,
    anchor_in, live_in, hidden_ref, grads_ref,
    feat_ref, wself_ref, wneigh_ref, bias_ref, cot_ref, hub_ref, rows_ref, count_ref, values_ref,
    target_ref, anchor_ref, live_ref,
    src_ref, full_ref, stacked, outbox, hub0, hub0_in, hub_parts, table, order, running,
    aggs, weights, bias, own_term, sums, pieces, inbox, partial, crossbox, totals,
    load_sem, table_sem, halo_send, halo_recv, feat_send, feat_recv, hub_send, hub_recv,
    agg_send, agg_recv, reduce_send, reduce_recv,
):
    me = lax.axis_index("nodes")
    feat = lax.axis_index("feat")
    core = me % 2
    z = (me // 2) % NZ
    x = me // (2 * NZ)
    loads = [
        started(pltpu.make_async_copy(src, dst, load_sem.at[i]))
        for i, (src, dst) in enumerate(
            (
                (feat_in, feat_ref), (rows_in, rows_ref), (hub_in, hub_ref), (count_in, count_ref),
                (target_in, target_ref), (anchor_in, anchor_ref), (live_in, live_ref),
                (wself_in, wself_ref), (wneigh_in, wneigh_ref), (bias_in, bias_ref),
                (cot_in, cot_ref), (values_in, values_ref),
            )
        )
    ]
    barrier = pltpu.get_barrier_semaphore()

    def node_signal(k, _):
        peer_signal(barrier, (me + k) % NN, feat)
        return 0

    lax.fori_loop(1, NN, node_signal, 0)
    for k in range(1, NF):
        peer_signal(barrier, me, (feat + k) % NF)

    for copy in loads[:4]:
        copy.wait()
    for h in range(16):
        stacked[h * 32 : (h + 1) * 32, :] = feat_ref[:, h * 256 : (h + 1) * 256]
    lane = lax.broadcasted_iota(I32, (1, 128), 1)

    def pick(indices):
        down256 = lax.broadcasted_iota(I32, (256, 256), 0)
        hots = [(down256 == (index & 255)).astype(F32).astype(BF16) for index in indices]
        parts = [jnp.dot(stacked[...], hot, preferred_element_type=F32) for hot in hots]
        picked = []
        for index, part in zip(indices, parts):
            high = index >> 8
            out = jnp.zeros((32, 256), F32)
            for h in range(16):
                out = jnp.where(high == h, part[h * 32 : (h + 1) * 32], out)
            picked.append(out.astype(BF16))
        return picked

    def fill(chips):
        indices = []
        for chip in chips:
            pair = [
                jnp.where(lane < count_ref[0, node], rows_ref[pl.ds(node, 1), :], -1)
                for node in (2 * chip, 2 * chip + 1)
            ]
            indices.append(jnp.concatenate(pair, axis=1))
        for chip, rows in zip(chips, pick(indices)):
            outbox[2 * chip] = rows[:, :128]
            outbox[2 * chip + 1] = rows[:, 128:]

    def halo_copy(node):
        return remote(
            outbox.at[node], src_ref.at[32 + me], halo_send.at[node], halo_recv.at[me], node, feat
        )

    def chip_at(k, dz):
        dx = 2 + (1 - 2 * (k % 2)) * ((k + 1) // 2)
        return ((x + dx) % NX) * NZ + (z + dz) % NZ

    def send(chip):
        halo_copy(2 * chip).start()
        halo_copy(2 * chip + 1).start()

    def between_chips(i):
        return [
            chip_at(2 * (i % 2) + j // 2, 4 + (2 * (j % 2) - 1) * (1 + i // 2)) for j in range(4)
        ]

    def between(i, _):
        chips = between_chips(i)
        fill(chips)
        for chip in chips:
            send(chip)
        return 0

    sibling = me + 1 - 2 * core
    hubs = jnp.concatenate([hub_ref[...]] * 4, axis=1)
    hubs = jnp.where(lane // 32 % 2 == core, hubs, -1)
    own_hubs = pick([jnp.concatenate([hubs, jnp.full_like(hubs, -1)], axis=1)])[0][:, :128]
    hub0[...] = jnp.where(lane < 64, own_hubs[:16], own_hubs[16:])
    src_ref[32 + me] = jnp.zeros((32, 128), BF16)
    opposite = [chip_at(k, 4) for k in range(4)]
    fill(opposite)
    pl.semaphore_wait(barrier, NN - 1 + NF - 1)

    first = started(remote(hub0, hub0_in, hub_send.at[0], hub_recv.at[0], sibling, feat))
    feat_copies = [
        started(
            remote(
                feat_ref, full_ref.at[feat], feat_send.at[k], feat_recv.at[k], me,
                (feat + k) % NF,
            )
        )
        for k in range(1, NF)
    ]
    for chip in opposite:
        send(chip)
    lax.fori_loop(0, 1, between, 0)
    first.wait()
    hub_parts[x, z] = hub0[...] + hub0_in[...]

    def chip_hubs(k, zz):
        return remote(
            hub_parts.at[x, z], hub_parts.at[x, zz], hub_send.at[k], hub_recv.at[k],
            x * 2 * NZ + ((z + k) % NZ) * 2 + core, feat,
        )

    for k in FAR_FIRST:
        chip_hubs(k, z).start()
    lax.fori_loop(1, 6, between, 0)
    level = [chip_at(k, 0) for k in range(3)] + [me // 2]
    fill(level)
    for chip in level[:3]:
        send(chip)
    halo_copy(sibling).start()

    for copy in loads[4:-1]:
        copy.wait()
    down = lax.broadcasted_iota(I32, (TILES, TILES), 0)
    along = lax.broadcasted_iota(I32, (TILES, TILES), 1)
    slot_row = lax.broadcasted_iota(I32, (1, TILES), 1)
    key_row = jnp.where(slot_row < live_ref[0], jnp.clip(target_ref[...], 0, BLOCKS - 1), BLOCKS)
    anchor_row = jnp.clip(anchor_ref[...], 0, 111)

    def column(row):
        return jnp.sum(jnp.where(down == along, row, 0), axis=1, keepdims=True)

    key = column(key_row)
    ahead = (key_row < key) | ((key_row == key) & (along < down))
    rank = jnp.sum(jnp.where(ahead, 1, 0), axis=1, keepdims=True)
    placed = rank == along

    def sorted_row(col):
        return jnp.sum(jnp.where(placed, col, 0), axis=0, keepdims=True)

    key_sorted = sorted_row(key)
    slot_col = lax.broadcasted_iota(I32, (TILES, 1), 0)
    table[0:1, 0:TILES] = sorted_row(slot_col)
    table[1:2, 0:TILES] = sorted_row(column(anchor_row))
    table[2:3, 0:TILES] = key_sorted
    blocks_along = lax.broadcasted_iota(I32, (TILES, 128), 1)
    table[3:4, 0:128] = jnp.maximum(
        jnp.sum(jnp.where(key <= blocks_along, 1, 0), axis=0, keepdims=True) - 1, 0
    )
    to_scalars = started(pltpu.make_async_copy(table, order, table_sem))

    for k in range(1, NZ):
        chip_hubs(k, (z - k) % NZ).wait()

    def row_hubs(k, xx):
        return remote(
            hub_parts.at[x], hub_parts.at[xx], hub_send.at[7 + k], hub_recv.at[7 + k],
            ((x + k) % NX) * 2 * NZ + z * 2 + core, feat,
        )

    for k in (2, 1, 3):
        row_hubs(k, x).start()

    def mine(ref):
        part = ref[:, 0:64]
        for k in range(1, NF):
            part = jnp.where(feat == k, ref[:, k * 64 : (k + 1) * 64], part)
        return part

    weights[0] = mine(wself_ref).T
    weights[1] = mine(wneigh_ref).T
    bias[...] = jnp.broadcast_to(mine(bias_ref), (128, 64)).T
    sums[...] = jnp.zeros_like(sums)
    for b in range(32):
        src_ref[b] = feat_ref[:, b * 128 : (b + 1) * 128]
    full_ref[feat] = feat_ref[...]
    to_scalars.wait()
    loads[-1].wait()

    def flip(b, _):
        tiles = [values_ref[b * FLIPS + j].T for j in range(FLIPS)]
        for j in range(FLIPS):
            values_ref[b * FLIPS + j] = tiles[j]
        return 0

    lax.fori_loop(0, TILES // FLIPS, flip, 0)
    for k in range(1, NX):
        row_hubs(k, (x - k) % NX).wait()
    for b in range(16):
        even = hub_parts[b // 4, 2 * (b % 4)]
        odd = hub_parts[b // 4, 2 * (b % 4) + 1]
        src_ref[96 + b, 0:16, :] = jnp.concatenate([even[:, :64], odd[:, :64]], axis=1)
        src_ref[96 + b, 16:32, :] = jnp.concatenate([even[:, 64:], odd[:, 64:]], axis=1)

    def arrived(node):
        remote(
            outbox.at[node], src_ref.at[32 + node], halo_send.at[node], halo_recv.at[node], node,
            feat,
        ).wait_recv()

    def between_arrived(i, _):
        for chip in between_chips(i):
            arrived(2 * chip)
            arrived(2 * chip + 1)
        return 0

    for chip in opposite:
        arrived(2 * chip)
        arrived(2 * chip + 1)
    lax.fori_loop(0, 6, between_arrived, 0)
    for chip in level[:3]:
        arrived(2 * chip)
        arrived(2 * chip + 1)
    arrived(sibling)

    empty = jnp.zeros((32, 128), BF16)

    def batch(b, total):
        products = []
        for j in range(0, UNROLL, 2):
            slot = b * UNROLL + j
            one = src_ref[order[1, slot]]
            two = src_ref[order[1, slot + 1]]
            rows = jnp.concatenate(
                [jnp.concatenate([one, empty], axis=1), jnp.concatenate([empty, two], axis=1)],
                axis=0,
            )
            pair = jnp.concatenate(
                [values_ref[order[0, slot]], values_ref[order[0, slot + 1]]], axis=0
            )
            product = jnp.dot(rows, pair, preferred_element_type=F32)
            products += [product[:32], product[32:]]
        for j in range(UNROLL):
            slot = b * UNROLL + j
            same = order[2, slot] == order[2, jnp.maximum(slot - 1, 0)]
            total = jnp.where(same, total, 0.0) + products[j]
            running[slot] = total
        return total

    lax.fori_loop(0, TILES // UNROLL, batch, jnp.zeros((32, 128), F32))

    width = cot_ref.shape[1] // PARTS

    def at(c):
        return pl.ds(pl.multiple_of(c * width, width), width)

    def direct(c, way):
        slot = (1 - way) // 2
        own = aggs.at[c, feat]
        return remote(
            own, own, agg_send.at[slot, c], agg_recv.at[slot, c], me, (feat + way) % NF
        )

    def relay(c):
        way = 1 - 2 * (c % 2)
        theirs = aggs.at[c, (feat - way) % NF]
        return remote(
            theirs, theirs, agg_send.at[2, c], agg_recv.at[2, c], me, (feat + way) % NF
        )

    def over(c):
        own = aggs.at[c, feat]
        return remote(own, own, agg_send.at[2, c], agg_recv.at[2, c], me, (feat + 2) % NF)

    def give(c, _):
        ends = [running[order[3, c * 4 + k]].astype(BF16) for k in range(4)]
        aggs[c, feat] = jnp.concatenate(ends, axis=1)

        return 0

    def give_all(c, _):
        give(c, 0)
        over(c).start()
        direct(c, 1).start()
        direct(c, -1).start()
        return 0

    def give_near(c, _):
        give(c, 0)
        direct(c, 1).start()
        direct(c, -1).start()
        return 0

    lax.fori_loop(RELAYED, PARTS, give_all, 0)
    lax.fori_loop(0, RELAYED, give_near, 0)

    def halo_left(k, _):
        halo_copy((me + k) % NN).wait_send()
        return 0

    lax.fori_loop(1, NN, halo_left, 0)
    for copy in feat_copies:
        copy.wait()

    def own_part(c, _):
        own = full_ref[:, :, at(c)].reshape(128, width)
        own_term[:, at(c)] = (
            jnp.dot(weights[0], own, preferred_element_type=F32) + bias[:, 0:1]
        )
        return 0

    def columns(c):
        span = at(c)
        relay(c).wait_recv()
        own = full_ref[:, :, span].reshape(128, width)
        neigh = aggs[c].reshape(128, width)
        pre = own_term[:, span] + jnp.dot(weights[1], neigh, preferred_element_type=F32)
        gate = jax.nn.sigmoid(pre)
        hidden_ref[:, span] = (pre * gate).astype(BF16)
        grad = (cot_ref[:, span].astype(F32) * gate * (1.0 + pre * (1.0 - gate))).astype(BF16)
        every = jnp.concatenate([own, neigh, jnp.ones((128, width), BF16)], axis=0)
        sums[...] += lax.dot_general(grad, every, LAST, preferred_element_type=F32)

    def pass_on(c, _):
        direct(c, 1).wait_recv()
        direct(c, -1).wait_recv()
        relay(c).start()
        return 0

    def final(c, _):
        columns(c)
        return 0

    def drain(c, _):
        direct(c, 1).wait_send()
        direct(c, -1).wait_send()
        relay(c).wait_send()
        return 0

    lax.fori_loop(0, PARTS, own_part, 0)
    lax.fori_loop(0, RELAYED, pass_on, 0)
    for c in range(RELAYED, PARTS):
        direct(c, 1).wait_recv()
        direct(c, -1).wait_recv()
    lax.fori_loop(RELAYED, PARTS, final, 0)
    lax.fori_loop(0, RELAYED, final, 0)

    group = x * 2 + core

    def mate(j):
        return (j // 2) * 2 * NZ + z * 2 + j % 2

    def across(zz):
        return x * 2 * NZ + zz * 2 + core

    for j in range(8):
        pieces[j] = sums[8 * j : 8 * j + 8, :]
    own_piece = pieces.at[group]

    def scatter(k):
        j = (group + k) % 8
        return remote(
            pieces.at[j], inbox.at[group], reduce_send.at[0, j], reduce_recv.at[0, group],
            mate(j), feat,
        )

    def scatter_in(k):
        j = (group + k) % 8
        return remote(
            pieces.at[j], inbox.at[j], reduce_send.at[0, j], reduce_recv.at[0, j], mate(j), feat
        )

    for k in FAR_FIRST:
        scatter(k).start()
    inbox[group] = own_piece[...]
    lax.fori_loop(0, PARTS, drain, 0)
    for k in range(1, 8):
        scatter_in(k).wait()
    crossed = inbox[0]
    for j in range(1, 8):
        crossed = crossed + inbox[j]
    partial[...] = crossed
    crossbox[z] = crossed

    def cross(k):
        zz = (z + k) % NZ
        return remote(
            partial, crossbox.at[z], reduce_send.at[1, zz], reduce_recv.at[1, z], across(zz), feat
        )

    def cross_in(k):
        zz = (z + k) % NZ
        return remote(
            partial, crossbox.at[zz], reduce_send.at[1, zz], reduce_recv.at[1, zz], across(zz),
            feat,
        )

    for k in FAR_FIRST:
        cross(k).start()
    for k in range(1, 8):
        cross_in(k).wait()
    total = crossbox[0]
    for j in range(1, 8):
        total = total + crossbox[j]
    totals[group] = total

    def spread(k):
        j = (group + k) % 8
        return remote(
            totals.at[group], totals.at[group], reduce_send.at[2, j], reduce_recv.at[2, group],
            mate(j), feat,
        )

    def spread_in(k):
        j = (group + k) % 8
        return remote(
            totals.at[group], totals.at[j], reduce_send.at[2, j], reduce_recv.at[2, j], mate(j),
            feat,
        )

    for k in FAR_FIRST:
        spread(k).start()
    for k in range(1, 8):
        spread_in(k).wait()
    grads_ref[...] = totals[...].reshape(64, 384)


def finish_kernel(hidden_ref, grads_ref, hidden_out, gself_out, gneigh_out, gbias_out, bias, sem):
    copies = [
        started(pltpu.make_async_copy(src, dst, sem.at[i]))
        for i, (src, dst) in enumerate(
            (
                (hidden_ref, hidden_out), (grads_ref.at[:, 0:128], gself_out),
                (grads_ref.at[:, 128:256], gneigh_out),
            )
        )
    ]
    bias[...] = grads_ref[:, 256:384].T[0:1, :]
    copies.append(started(pltpu.make_async_copy(bias, gbias_out, sem.at[3])))
    for copy in copies:
        copy.wait()


def local(
    features, w_self, w_neigh, hidden_bias, cotangent, hub_local, send_rows, send_count,
    tile_values, tile_target, tile_anchor, tile_count,
):
    cols = features.shape[1]
    operands = (
        features, w_self, w_neigh, hidden_bias.reshape(1, -1), cotangent, hub_local, send_rows[0],
        send_count, tile_values, tile_target, tile_anchor,
    )
    operands = tuple(
        pltpu.with_memory_space_constraint(operand, pltpu.MemorySpace.HBM) for operand in operands
    ) + (tile_count,)
    vmem = pl.BlockSpec(memory_space=pltpu.VMEM)
    scalars = (7, 11)
    hidden, grads = pl.pallas_call(
        layer_kernel,
        name="layer",
        out_shape=(
            jax.ShapeDtypeStruct((64, cols), BF16),
            jax.ShapeDtypeStruct((64, 384), F32),
        ),
        in_specs=[pl.BlockSpec(memory_space=pl.ANY)] * 12,
        out_specs=(vmem,) * 2,
        scratch_shapes=[
            (pltpu.SMEM if i in scalars else pltpu.VMEM)(operand.shape, operand.dtype)
            for i, operand in enumerate(operands)
        ]
        + [
            pltpu.VMEM((112, 32, 128), BF16),
            pltpu.VMEM((NF, 32, cols), BF16),
            pltpu.VMEM((512, 256), BF16),
            pltpu.VMEM((NN, 32, 128), BF16),
            pltpu.VMEM((16, 128), BF16),
            pltpu.VMEM((16, 128), BF16),
            pltpu.VMEM((NX, NZ, 16, 128), BF16),
            pltpu.VMEM((8, 384), I32),
            pltpu.SMEM((8, 384), I32),
            pltpu.VMEM((TILES, 32, 128), F32),
            pltpu.VMEM((PARTS, NF, 32, cols // PARTS), BF16),
            pltpu.VMEM((2, 64, 128), BF16),
            pltpu.VMEM((64, 128), F32),
            pltpu.VMEM((64, cols), F32),
            pltpu.VMEM((64, 384), F32),
            pltpu.VMEM((8, 8, 384), F32),
            pltpu.VMEM((8, 8, 384), F32),
            pltpu.VMEM((8, 384), F32),
            pltpu.VMEM((8, 8, 384), F32),
            pltpu.VMEM((8, 8, 384), F32),
            pltpu.SemaphoreType.DMA((12,)),
            pltpu.SemaphoreType.DMA,
            pltpu.SemaphoreType.DMA((NN,)),
            pltpu.SemaphoreType.DMA((NN,)),
            pltpu.SemaphoreType.DMA((NF,)),
            pltpu.SemaphoreType.DMA((NF,)),
            pltpu.SemaphoreType.DMA((11,)),
            pltpu.SemaphoreType.DMA((11,)),
            pltpu.SemaphoreType.DMA((3, PARTS)),
            pltpu.SemaphoreType.DMA((3, PARTS)),
            pltpu.SemaphoreType.DMA((3, 8)),
            pltpu.SemaphoreType.DMA((3, 8)),
        ],
        compiler_params=pltpu.CompilerParams(
            collective_id=0, has_side_effects=True, vmem_limit_bytes=40 * 2**20
        ),
    )(*operands)
    hidden, grad_self, grad_neigh, bias_grad = pl.pallas_call(
        finish_kernel,
        name="finish",
        out_shape=(
            jax.ShapeDtypeStruct((64, cols), BF16),
            jax.ShapeDtypeStruct((64, 128), F32),
            jax.ShapeDtypeStruct((64, 128), F32),
            jax.ShapeDtypeStruct((1, 64), F32),
        ),
        in_specs=[vmem] * 2,
        out_specs=(pl.BlockSpec(memory_space=pl.ANY),) * 4,
        scratch_shapes=[pltpu.VMEM((1, 64), F32), pltpu.SemaphoreType.DMA((4,))],
        compiler_params=pltpu.CompilerParams(vmem_limit_bytes=4 * 2**20),
    )(hidden, grads)
    return hidden, grad_self.T, grad_neigh.T, bias_grad.reshape(-1)


def solution(mesh):
    in_specs = (
        P("feat", "nodes"), P(), P(), P(), P("feat", "nodes"), P("nodes", None),
        P("nodes", None, None), P("nodes", None), P("nodes", None, None), P("nodes", None),
        P("nodes", None), P("nodes"),
    )
    out_specs = (P("feat", "nodes"), P(None, "feat"), P(None, "feat"), P("feat"))
    return jax.shard_map(local, mesh=mesh, in_specs=in_specs, out_specs=out_specs, check_vma=False)
```

```python
import jax
import jax.numpy as jnp
from jax import lax
from jax.experimental import pallas as pl
from jax.experimental.pallas import tpu as pltpu
from jax.sharding import PartitionSpec as P

MESH = pl.DeviceIdType.MESH
NX, NZ, NN, NF = 4, 8, 64, 4
TILES = 352
BLOCKS = 32
UNROLL = 88
FLIPS = 16
FAR_FIRST = (4, 3, 5, 2, 6, 1, 7)
PARTS = 8
RELAYED = 6
LAST = (((1,), (1,)), ((), ()))
F32 = jnp.float32
BF16 = jnp.bfloat16
I32 = jnp.int32


def peer_signal(barrier, node, part):
    pl.semaphore_signal(
        barrier, inc=1, device_id={"nodes": node, "feat": part}, device_id_type=MESH
    )


def remote(src, dst, send_sem, recv_sem, node, part):
    return pltpu.make_async_remote_copy(
        src_ref=src, dst_ref=dst, send_sem=send_sem, recv_sem=recv_sem,
        device_id={"nodes": node, "feat": part}, device_id_type=MESH,
    )


def started(copy):
    copy.start()
    return copy


def layer_kernel(
    feat_in, wself_in, wneigh_in, bias_in, cot_in, hub_in, rows_in, count_in, values_in, target_in,
    anchor_in, live_in, hidden_ref, grads_ref,
    feat_ref, wself_ref, wneigh_ref, bias_ref, cot_ref, hub_ref, rows_ref, count_ref, values_ref,
    target_ref, anchor_ref, live_ref,
    src_ref, full_ref, stacked, outbox, hub0, hub0_in, hub_parts, table, order, running,
    aggs, weights, bias, own_term, sums, pieces, inbox, partial, crossbox, totals,
    load_sem, table_sem, halo_send, halo_recv, feat_send, feat_recv, hub_send, hub_recv,
    agg_send, agg_recv, reduce_send, reduce_recv,
):
    me = lax.axis_index("nodes")
    feat = lax.axis_index("feat")
    core = me % 2
    z = (me // 2) % NZ
    x = me // (2 * NZ)
    loads = [
        pltpu.make_async_copy(src, dst, load_sem.at[i])
        for i, (src, dst) in enumerate(
            (
                (feat_in, feat_ref), (rows_in, rows_ref), (hub_in, hub_ref), (count_in, count_ref),
                (target_in, target_ref), (anchor_in, anchor_ref), (live_in, live_ref),
                (wself_in, wself_ref), (wneigh_in, wneigh_ref), (bias_in, bias_ref),
                (cot_in, cot_ref), (values_in, values_ref),
            )
        )
    ]
    for copy in loads[:4]:
        copy.start()
    def chip_at(k, dz):
        dx = 2 + (1 - 2 * (k % 2)) * ((k + 1) // 2)
        return ((x + dx) % NX) * NZ + (z + dz) % NZ

    def between_chips(i):
        return [
            chip_at(2 * (i % 2) + j // 2, 4 + (2 * (j % 2) - 1) * (1 + i // 2)) for j in range(4)
        ]

    opposite = [chip_at(k, 4) for k in range(4)]
    level = [chip_at(k, 0) for k in range(3)] + [me // 2]
    sibling = me + 1 - 2 * core
    barrier = pltpu.get_barrier_semaphore()

    def greet(chip):
        peer_signal(barrier, 2 * chip, feat)
        peer_signal(barrier, 2 * chip + 1, feat)

    def between_greet(i, _):
        for chip in between_chips(i):
            greet(chip)
        return 0

    for chip in opposite:
        greet(chip)
    lax.fori_loop(0, 6, between_greet, 0)
    for k in range(1, NF):
        peer_signal(barrier, me, (feat + k) % NF)
    for chip in level[:3]:
        greet(chip)
    peer_signal(barrier, sibling, feat)
    for copy in loads[4:]:
        copy.start()

    for copy in loads[:4]:
        copy.wait()
    for h in range(16):
        stacked[h * 32 : (h + 1) * 32, :] = feat_ref[:, h * 256 : (h + 1) * 256]
    lane = lax.broadcasted_iota(I32, (1, 128), 1)

    def pick(indices):
        down256 = lax.broadcasted_iota(I32, (256, 256), 0)
        hots = [(down256 == (index & 255)).astype(F32).astype(BF16) for index in indices]
        parts = [jnp.dot(stacked[...], hot, preferred_element_type=F32) for hot in hots]
        picked = []
        for index, part in zip(indices, parts):
            high = index >> 8
            out = jnp.zeros((32, 256), F32)
            for h in range(16):
                out = jnp.where(high == h, part[h * 32 : (h + 1) * 32], out)
            picked.append(out.astype(BF16))
        return picked

    def fill(chips):
        indices = []
        for chip in chips:
            pair = [
                jnp.where(lane < count_ref[0, node], rows_ref[pl.ds(node, 1), :], -1)
                for node in (2 * chip, 2 * chip + 1)
            ]
            indices.append(jnp.concatenate(pair, axis=1))
        for chip, rows in zip(chips, pick(indices)):
            outbox[2 * chip] = rows[:, :128]
            outbox[2 * chip + 1] = rows[:, 128:]

    def halo_copy(node):
        return remote(
            outbox.at[node], src_ref.at[32 + me], halo_send.at[node], halo_recv.at[me], node, feat
        )

    def send(chip):
        halo_copy(2 * chip).start()
        halo_copy(2 * chip + 1).start()

    def between(i, _):
        chips = between_chips(i)
        fill(chips)
        for chip in chips:
            send(chip)
        return 0

    hubs = jnp.concatenate([hub_ref[...]] * 4, axis=1)
    hubs = jnp.where(lane // 32 % 2 == core, hubs, -1)
    own_hubs = pick([jnp.concatenate([hubs, jnp.full_like(hubs, -1)], axis=1)])[0][:, :128]
    hub0[...] = jnp.where(lane < 64, own_hubs[:16], own_hubs[16:])
    src_ref[32 + me] = jnp.zeros((32, 128), BF16)
    fill(opposite)
    pl.semaphore_wait(barrier, NN - 1 + NF - 1)

    first = started(remote(hub0, hub0_in, hub_send.at[0], hub_recv.at[0], sibling, feat))
    feat_copies = [
        started(
            remote(
                feat_ref, full_ref.at[feat], feat_send.at[k], feat_recv.at[k], me,
                (feat + k) % NF,
            )
        )
        for k in range(1, NF)
    ]
    for chip in opposite:
        send(chip)
    lax.fori_loop(0, 1, between, 0)
    first.wait()
    hub_parts[x, z] = hub0[...] + hub0_in[...]

    def chip_hubs(k, zz):
        return remote(
            hub_parts.at[x, z], hub_parts.at[x, zz], hub_send.at[k], hub_recv.at[k],
            x * 2 * NZ + ((z + k) % NZ) * 2 + core, feat,
        )

    for k in FAR_FIRST:
        chip_hubs(k, z).start()
    lax.fori_loop(1, 6, between, 0)
    fill(level)
    for chip in level[:3]:
        send(chip)
    halo_copy(sibling).start()

    for copy in loads[4:-1]:
        copy.wait()
    down = lax.broadcasted_iota(I32, (TILES, TILES), 0)
    along = lax.broadcasted_iota(I32, (TILES, TILES), 1)
    slot_row = lax.broadcasted_iota(I32, (1, TILES), 1)
    key_row = jnp.where(slot_row < live_ref[0], jnp.clip(target_ref[...], 0, BLOCKS - 1), BLOCKS)
    anchor_row = jnp.clip(anchor_ref[...], 0, 111)

    def column(row):
        return jnp.sum(jnp.where(down == along, row, 0), axis=1, keepdims=True)

    key = column(key_row)
    ahead = (key_row < key) | ((key_row == key) & (along < down))
    rank = jnp.sum(jnp.where(ahead, 1, 0), axis=1, keepdims=True)
    placed = rank == along

    def sorted_row(col):
        return jnp.sum(jnp.where(placed, col, 0), axis=0, keepdims=True)

    key_sorted = sorted_row(key)
    slot_col = lax.broadcasted_iota(I32, (TILES, 1), 0)
    table[0:1, 0:TILES] = sorted_row(slot_col)
    table[1:2, 0:TILES] = sorted_row(column(anchor_row))
    table[2:3, 0:TILES] = key_sorted
    blocks_along = lax.broadcasted_iota(I32, (TILES, 128), 1)
    table[3:4, 0:128] = jnp.maximum(
        jnp.sum(jnp.where(key <= blocks_along, 1, 0), axis=0, keepdims=True) - 1, 0
    )
    to_scalars = started(pltpu.make_async_copy(table, order, table_sem))

    for k in range(1, NZ):
        chip_hubs(k, (z - k) % NZ).wait()

    def row_hubs(k, xx):
        return remote(
            hub_parts.at[x], hub_parts.at[xx], hub_send.at[7 + k], hub_recv.at[7 + k],
            ((x + k) % NX) * 2 * NZ + z * 2 + core, feat,
        )

    for k in (2, 1, 3):
        row_hubs(k, x).start()

    def mine(ref):
        part = ref[:, 0:64]
        for k in range(1, NF):
            part = jnp.where(feat == k, ref[:, k * 64 : (k + 1) * 64], part)
        return part

    weights[0] = mine(wself_ref).T
    weights[1] = mine(wneigh_ref).T
    bias[...] = jnp.broadcast_to(mine(bias_ref), (128, 64)).T
    sums[...] = jnp.zeros_like(sums)
    for b in range(32):
        src_ref[b] = feat_ref[:, b * 128 : (b + 1) * 128]
    full_ref[feat] = feat_ref[...]
    to_scalars.wait()
    loads[-1].wait()

    def flip(b, _):
        tiles = [values_ref[b * FLIPS + j].T for j in range(FLIPS)]
        for j in range(FLIPS):
            values_ref[b * FLIPS + j] = tiles[j]
        return 0

    lax.fori_loop(0, TILES // FLIPS, flip, 0)
    for k in range(1, NX):
        row_hubs(k, (x - k) % NX).wait()
    for b in range(16):
        even = hub_parts[b // 4, 2 * (b % 4)]
        odd = hub_parts[b // 4, 2 * (b % 4) + 1]
        src_ref[96 + b, 0:16, :] = jnp.concatenate([even[:, :64], odd[:, :64]], axis=1)
        src_ref[96 + b, 16:32, :] = jnp.concatenate([even[:, 64:], odd[:, 64:]], axis=1)

    def arrived(node):
        remote(
            outbox.at[node], src_ref.at[32 + node], halo_send.at[node], halo_recv.at[node], node,
            feat,
        ).wait_recv()

    def between_arrived(i, _):
        for chip in between_chips(i):
            arrived(2 * chip)
            arrived(2 * chip + 1)
        return 0

    for chip in opposite:
        arrived(2 * chip)
        arrived(2 * chip + 1)
    lax.fori_loop(0, 6, between_arrived, 0)
    for chip in level[:3]:
        arrived(2 * chip)
        arrived(2 * chip + 1)
    arrived(sibling)

    empty = jnp.zeros((32, 128), BF16)

    def batch(b, total):
        products = []
        for j in range(0, UNROLL, 2):
            slot = b * UNROLL + j
            one = src_ref[order[1, slot]]
            two = src_ref[order[1, slot + 1]]
            rows = jnp.concatenate(
                [jnp.concatenate([one, empty], axis=1), jnp.concatenate([empty, two], axis=1)],
                axis=0,
            )
            pair = jnp.concatenate(
                [values_ref[order[0, slot]], values_ref[order[0, slot + 1]]], axis=0
            )
            product = jnp.dot(rows, pair, preferred_element_type=F32)
            products += [product[:32], product[32:]]
        for j in range(UNROLL):
            slot = b * UNROLL + j
            same = order[2, slot] == order[2, jnp.maximum(slot - 1, 0)]
            total = jnp.where(same, total, 0.0) + products[j]
            running[slot] = total
        return total

    lax.fori_loop(0, TILES // UNROLL, batch, jnp.zeros((32, 128), F32))

    width = cot_ref.shape[1] // PARTS

    def at(c):
        return pl.ds(pl.multiple_of(c * width, width), width)

    def direct(c, way):
        slot = (1 - way) // 2
        own = aggs.at[c, feat]
        return remote(
            own, own, agg_send.at[slot, c], agg_recv.at[slot, c], me, (feat + way) % NF
        )

    def relay(c):
        way = 1 - 2 * (c % 2)
        theirs = aggs.at[c, (feat - way) % NF]
        return remote(
            theirs, theirs, agg_send.at[2, c], agg_recv.at[2, c], me, (feat + way) % NF
        )

    def over(c):
        own = aggs.at[c, feat]
        return remote(own, own, agg_send.at[2, c], agg_recv.at[2, c], me, (feat + 2) % NF)

    def give(c, _):
        ends = [running[order[3, c * 4 + k]].astype(BF16) for k in range(4)]
        aggs[c, feat] = jnp.concatenate(ends, axis=1)

        return 0

    def give_all(c, _):
        give(c, 0)
        over(c).start()
        direct(c, 1).start()
        direct(c, -1).start()
        return 0

    def give_near(c, _):
        give(c, 0)
        direct(c, 1).start()
        direct(c, -1).start()
        return 0

    lax.fori_loop(RELAYED, PARTS, give_all, 0)
    lax.fori_loop(0, RELAYED, give_near, 0)

    def halo_left(k, _):
        halo_copy((me + k) % NN).wait_send()
        return 0

    lax.fori_loop(1, NN, halo_left, 0)
    for copy in feat_copies:
        copy.wait()

    def own_part(c, _):
        own = full_ref[:, :, at(c)].reshape(128, width)
        own_term[:, at(c)] = (
            jnp.dot(weights[0], own, preferred_element_type=F32) + bias[:, 0:1]
        )
        return 0

    def columns(c):
        span = at(c)
        relay(c).wait_recv()
        own = full_ref[:, :, span].reshape(128, width)
        neigh = aggs[c].reshape(128, width)
        pre = own_term[:, span] + jnp.dot(weights[1], neigh, preferred_element_type=F32)
        gate = jax.nn.sigmoid(pre)
        hidden_ref[:, span] = (pre * gate).astype(BF16)
        grad = (cot_ref[:, span].astype(F32) * gate * (1.0 + pre * (1.0 - gate))).astype(BF16)
        every = jnp.concatenate([own, neigh, jnp.ones((128, width), BF16)], axis=0)
        sums[...] += lax.dot_general(grad, every, LAST, preferred_element_type=F32)

    def pass_on(c, _):
        direct(c, 1).wait_recv()
        direct(c, -1).wait_recv()
        relay(c).start()
        return 0

    def final(c, _):
        columns(c)
        return 0

    def drain(c, _):
        direct(c, 1).wait_send()
        direct(c, -1).wait_send()
        relay(c).wait_send()
        return 0

    lax.fori_loop(0, PARTS, own_part, 0)
    lax.fori_loop(0, RELAYED, pass_on, 0)
    for c in range(RELAYED, PARTS):
        direct(c, 1).wait_recv()
        direct(c, -1).wait_recv()
    lax.fori_loop(RELAYED, PARTS, final, 0)
    lax.fori_loop(0, RELAYED, final, 0)

    group = x * 2 + core

    def mate(j):
        return (j // 2) * 2 * NZ + z * 2 + j % 2

    def across(zz):
        return x * 2 * NZ + zz * 2 + core

    for j in range(8):
        pieces[j] = sums[8 * j : 8 * j + 8, :]
    own_piece = pieces.at[group]

    def scatter(k):
        j = (group + k) % 8
        return remote(
            pieces.at[j], inbox.at[group], reduce_send.at[0, j], reduce_recv.at[0, group],
            mate(j), feat,
        )

    def scatter_in(k):
        j = (group + k) % 8
        return remote(
            pieces.at[j], inbox.at[j], reduce_send.at[0, j], reduce_recv.at[0, j], mate(j), feat
        )

    for k in FAR_FIRST:
        scatter(k).start()
    inbox[group] = own_piece[...]
    lax.fori_loop(0, PARTS, drain, 0)
    for k in range(1, 8):
        scatter_in(k).wait()
    crossed = inbox[0]
    for j in range(1, 8):
        crossed = crossed + inbox[j]
    partial[...] = crossed
    crossbox[z] = crossed

    def cross(k):
        zz = (z + k) % NZ
        return remote(
            partial, crossbox.at[z], reduce_send.at[1, zz], reduce_recv.at[1, z], across(zz), feat
        )

    def cross_in(k):
        zz = (z + k) % NZ
        return remote(
            partial, crossbox.at[zz], reduce_send.at[1, zz], reduce_recv.at[1, zz], across(zz),
            feat,
        )

    for k in FAR_FIRST:
        cross(k).start()
    for k in range(1, 8):
        cross_in(k).wait()
    total = crossbox[0]
    for j in range(1, 8):
        total = total + crossbox[j]
    totals[group] = total

    def spread(k):
        j = (group + k) % 8
        return remote(
            totals.at[group], totals.at[group], reduce_send.at[2, j], reduce_recv.at[2, group],
            mate(j), feat,
        )

    def spread_in(k):
        j = (group + k) % 8
        return remote(
            totals.at[group], totals.at[j], reduce_send.at[2, j], reduce_recv.at[2, j], mate(j),
            feat,
        )

    for k in FAR_FIRST:
        spread(k).start()
    for k in range(1, 8):
        spread_in(k).wait()
    grads_ref[...] = totals[...].reshape(64, 384)


def finish_kernel(hidden_ref, grads_ref, hidden_out, gself_out, gneigh_out, gbias_out, bias, sem):
    copies = [
        started(pltpu.make_async_copy(src, dst, sem.at[i]))
        for i, (src, dst) in enumerate(
            (
                (hidden_ref, hidden_out), (grads_ref.at[:, 0:128], gself_out),
                (grads_ref.at[:, 128:256], gneigh_out),
            )
        )
    ]
    bias[...] = grads_ref[:, 256:384].T[0:1, :]
    copies.append(started(pltpu.make_async_copy(bias, gbias_out, sem.at[3])))
    for copy in copies:
        copy.wait()


def local(
    features, w_self, w_neigh, hidden_bias, cotangent, hub_local, send_rows, send_count,
    tile_values, tile_target, tile_anchor, tile_count,
):
    cols = features.shape[1]
    operands = (
        features, w_self, w_neigh, hidden_bias.reshape(1, -1), cotangent, hub_local, send_rows[0],
        send_count, tile_values, tile_target, tile_anchor,
    )
    operands = tuple(
        pltpu.with_memory_space_constraint(operand, pltpu.MemorySpace.HBM) for operand in operands
    ) + (tile_count,)
    vmem = pl.BlockSpec(memory_space=pltpu.VMEM)
    scalars = (7, 11)
    hidden, grads = pl.pallas_call(
        layer_kernel,
        name="layer",
        out_shape=(
            jax.ShapeDtypeStruct((64, cols), BF16),
            jax.ShapeDtypeStruct((64, 384), F32),
        ),
        in_specs=[pl.BlockSpec(memory_space=pl.ANY)] * 12,
        out_specs=(vmem,) * 2,
        scratch_shapes=[
            (pltpu.SMEM if i in scalars else pltpu.VMEM)(operand.shape, operand.dtype)
            for i, operand in enumerate(operands)
        ]
        + [
            pltpu.VMEM((112, 32, 128), BF16),
            pltpu.VMEM((NF, 32, cols), BF16),
            pltpu.VMEM((512, 256), BF16),
            pltpu.VMEM((NN, 32, 128), BF16),
            pltpu.VMEM((16, 128), BF16),
            pltpu.VMEM((16, 128), BF16),
            pltpu.VMEM((NX, NZ, 16, 128), BF16),
            pltpu.VMEM((8, 384), I32),
            pltpu.SMEM((8, 384), I32),
            pltpu.VMEM((TILES, 32, 128), F32),
            pltpu.VMEM((PARTS, NF, 32, cols // PARTS), BF16),
            pltpu.VMEM((2, 64, 128), BF16),
            pltpu.VMEM((64, 128), F32),
            pltpu.VMEM((64, cols), F32),
            pltpu.VMEM((64, 384), F32),
            pltpu.VMEM((8, 8, 384), F32),
            pltpu.VMEM((8, 8, 384), F32),
            pltpu.VMEM((8, 384), F32),
            pltpu.VMEM((8, 8, 384), F32),
            pltpu.VMEM((8, 8, 384), F32),
            pltpu.SemaphoreType.DMA((12,)),
            pltpu.SemaphoreType.DMA,
            pltpu.SemaphoreType.DMA((NN,)),
            pltpu.SemaphoreType.DMA((NN,)),
            pltpu.SemaphoreType.DMA((NF,)),
            pltpu.SemaphoreType.DMA((NF,)),
            pltpu.SemaphoreType.DMA((11,)),
            pltpu.SemaphoreType.DMA((11,)),
            pltpu.SemaphoreType.DMA((3, PARTS)),
            pltpu.SemaphoreType.DMA((3, PARTS)),
            pltpu.SemaphoreType.DMA((3, 8)),
            pltpu.SemaphoreType.DMA((3, 8)),
        ],
        compiler_params=pltpu.CompilerParams(
            collective_id=0, has_side_effects=True, vmem_limit_bytes=40 * 2**20
        ),
    )(*operands)
    hidden, grad_self, grad_neigh, bias_grad = pl.pallas_call(
        finish_kernel,
        name="finish",
        out_shape=(
            jax.ShapeDtypeStruct((64, cols), BF16),
            jax.ShapeDtypeStruct((64, 128), F32),
            jax.ShapeDtypeStruct((64, 128), F32),
            jax.ShapeDtypeStruct((1, 64), F32),
        ),
        in_specs=[vmem] * 2,
        out_specs=(pl.BlockSpec(memory_space=pl.ANY),) * 4,
        scratch_shapes=[pltpu.VMEM((1, 64), F32), pltpu.SemaphoreType.DMA((4,))],
        compiler_params=pltpu.CompilerParams(vmem_limit_bytes=4 * 2**20),
    )(hidden, grads)
    return hidden, grad_self.T, grad_neigh.T, bias_grad.reshape(-1)


def solution(mesh):
    in_specs = (
        P("feat", "nodes"), P(), P(), P(), P("feat", "nodes"), P("nodes", None),
        P("nodes", None, None), P("nodes", None), P("nodes", None, None), P("nodes", None),
        P("nodes", None), P("nodes"),
    )
    out_specs = (P("feat", "nodes"), P(None, "feat"), P(None, "feat"), P("feat"))
    return jax.shard_map(local, mesh=mesh, in_specs=in_specs, out_specs=out_specs, check_vma=False)
```
